256 devices in a mesh: row: 32 (over z, x), col: 4 (over y), depth: 2 (over core).
Axes of the slice: x: 4, y: 4, z: 8, core: 2. Of those that a mesh axis runs over, the one named last changes fastest.
Arguments:
- layer_input: bfloat16 [3072, 4096], P(('depth', 'col'), 'row'), may hold values from -1.796875 to 1.796875
- gate_pre: bfloat16 [3072, 14784], P(('depth', 'row'), 'col'), may hold values from -9 to 9
- up_pre: bfloat16 [3072, 14784], P(('depth', 'row'), 'col'), may hold values from -6 to 6
- hidden_grad: bfloat16 [3072, 14784], P(('depth', 'row'), 'col'), may hold values from -2.5 to 2.5
- gate_weight: bfloat16 [4096, 14784], P('row', 'col'), may hold values from -0.09375 to 0.09375
- up_weight: bfloat16 [4096, 14784], P('row', 'col'), may hold values from -0.09375 to 0.09375
Outputs:
- input_grad: bfloat16 [3072, 4096], P(('depth', 'col'), 'row')
- gate_weight_grad: bfloat16 [4096, 14784], P(('row', 'depth'), 'col')
- up_weight_grad: bfloat16 [4096, 14784], P(('row', 'depth'), 'col')
The draws below stay inside these ranges and needn't reach their ends.
All inputs are finite; a program needn't handle non-finite values.
Results may differ from the reference program's by a relative error of at most 0.014.
Values may be sent and summed in bfloat16 or wider, within the bound.
A program may use at most 128 MiB of HBM per device.

```python
import jax
import jax.numpy as jnp

D = 4096
FF = 14784
LAYER = 1536
TOKENS = 3072
N_COL = 4
N_DEPTH = 2


def spiked(drawn, rng, source, target, blocks, factor):
    def block_of(position):
        return (jnp.arange(drawn.shape[position]) // (drawn.shape[position] // blocks)).reshape((-1,) + (1,) * (drawn.ndim - 1 - position))

    first = jax.random.permutation(rng, blocks)[block_of(target)]
    second = (block_of(target) + blocks // 2) % blocks
    return jnp.where((block_of(source) == first) | (block_of(source) == second), factor * drawn, drawn)


def block_levels(rng, extent, pieces, least, high):
    level = 1.0
    for dim, blocks in pieces:
        heights = jax.random.uniform(jax.random.fold_in(jax.random.fold_in(rng, 6), dim), (blocks,), jnp.float32, least / len(pieces), high / len(pieces))
        level = level * jnp.repeat(jnp.exp(heights), extent[dim] // blocks).reshape((-1,) + (1,) * (len(extent) - 1 - dim))
    return level


def normal_values(rng, dims, scale, reach, shards=(), dtype=jnp.bfloat16):
    drawn = scale * jax.random.normal(rng, dims, jnp.float32)
    if shards:
        drawn = drawn * block_levels(rng, dims, shards, -0.22, 0.18)
    return jnp.clip(drawn, -reach, reach).astype(dtype)


def bell_draw_with(rng, dims, width, bound, split, heavy, kind=jnp.bfloat16):
    array = width * jax.random.normal(rng, dims, jnp.float32)
    if split:
        array = array * block_levels(rng, dims, split, -0.22, 0.18)
    return jnp.clip(spiked(array, jax.random.fold_in(rng, 3), *heavy), -bound, bound).astype(kind)


def setup_inputs(seed: int = 0) -> dict:
    splits = jax.random.split(jax.random.key(seed), 7)
    layer_input = bell_draw_with(splits[0], (TOKENS, D), 0.3, 1.796875, ((0, 8), (1, 32)), (0, 1, 32, 2.75))
    gate_pre = normal_values(splits[1], (TOKENS, FF), 1.5, 9.0, ((0, 64), (1, 4)))
    up_pre = normal_values(splits[2], (TOKENS, FF), 1.0, 6.0, ((0, 64), (1, 4)))
    hidden_grad = bell_draw_with(splits[3], (TOKENS, FF), 0.15, 2.5, ((0, 64), (1, 4)), (1, 0, 64, 4.0))
    gate_weight = normal_values(splits[4], (D, FF), D ** -0.5, 0.09375, ((0, 32), (1, 4)))
    up_weight = normal_values(splits[5], (D, FF), D ** -0.5, 0.09375, ((0, 32), (1, 4)))
    return dict(layer_input=layer_input, gate_pre=gate_pre, up_pre=up_pre, hidden_grad=hidden_grad, gate_weight=gate_weight, up_weight=up_weight)


def reference(layer_input, gate_pre, up_pre, hidden_grad, gate_weight, up_weight):
    gate_f = gate_pre.astype(jnp.float32)
    up_f = up_pre.astype(jnp.float32)
    grad_f = hidden_grad.astype(jnp.float32)
    sigma = jax.nn.sigmoid(gate_f)
    gate_grad = (grad_f * up_f * sigma * (1.0 + gate_f * (1.0 - sigma))).astype(jnp.bfloat16)
    up_grad = (grad_f * gate_f * sigma).astype(jnp.bfloat16)
    block = FF // N_COL
    input_sum = jnp.zeros((TOKENS, D), jnp.float32)
    for index in range(N_COL):
        lo = index * block
        part = jnp.dot(gate_grad[:, lo:lo + block], gate_weight[:, lo:lo + block].T, preferred_element_type=jnp.float32)
        part = part + jnp.dot(up_grad[:, lo:lo + block], up_weight[:, lo:lo + block].T, preferred_element_type=jnp.float32)
        input_sum = input_sum + part.astype(jnp.bfloat16).astype(jnp.float32)
    gate_sum = jnp.zeros((D, FF), jnp.float32)
    up_sum = jnp.zeros((D, FF), jnp.float32)
    for index in range(N_DEPTH):
        lo = index * LAYER
        rows_x = layer_input[lo:lo + LAYER].T
        gate_sum = gate_sum + jnp.dot(rows_x, gate_grad[lo:lo + LAYER], preferred_element_type=jnp.float32).astype(jnp.bfloat16).astype(jnp.float32)
        up_sum = up_sum + jnp.dot(rows_x, up_grad[lo:lo + LAYER], preferred_element_type=jnp.float32).astype(jnp.bfloat16).astype(jnp.float32)
    return input_sum.astype(jnp.bfloat16), gate_sum.astype(jnp.bfloat16), up_sum.astype(jnp.bfloat16)
```

```python
import jax
import jax.numpy as jnp
from jax import lax
from jax.sharding import PartitionSpec as P


def swiglu_back(gate_pre, up_pre, hidden_grad):
    gate_f = gate_pre.astype(jnp.float32)
    up_f = up_pre.astype(jnp.float32)
    grad_f = hidden_grad.astype(jnp.float32)
    sigma = jax.nn.sigmoid(gate_f)
    gate_grad = (grad_f * up_f * sigma * (1.0 + gate_f * (1.0 - sigma))).astype(jnp.bfloat16)
    up_grad = (grad_f * gate_f * sigma).astype(jnp.bfloat16)
    return (gate_grad, up_grad)


def on_device(layer_input, gate_pre, up_pre, hidden_grad, gate_weight, up_weight):
    gate_loc, up_loc = swiglu_back(gate_pre, up_pre, hidden_grad)
    gate_grad = lax.all_gather(gate_loc, "row", axis=0, tiled=True)
    up_grad = lax.all_gather(up_loc, "row", axis=0, tiled=True)
    layer_x = lax.all_gather(layer_input, "col", axis=0, tiled=True)
    gate_part = lax.dot_general(
        layer_x, gate_grad, (((0,), (0,)), ((), ())), preferred_element_type=jnp.float32
    ).astype(jnp.bfloat16)
    gate_sum = lax.psum_scatter(gate_part, "depth", scatter_dimension=0, tiled=True)
    term = lax.dot_general(
        gate_grad, gate_weight, (((1,), (1,)), ((), ())), preferred_element_type=jnp.float32
    )
    term = term + lax.dot_general(
        up_grad, up_weight, (((1,), (1,)), ((), ())), preferred_element_type=jnp.float32
    )
    input_grad = lax.psum_scatter(term.astype(jnp.bfloat16), "col", scatter_dimension=0, tiled=True)
    up_part = lax.dot_general(
        layer_x, up_grad, (((0,), (0,)), ((), ())), preferred_element_type=jnp.float32
    ).astype(jnp.bfloat16)
    up_sum = lax.psum_scatter(up_part, "depth", scatter_dimension=0, tiled=True)
    return (input_grad, gate_sum, up_sum)


def solution(mesh):
    placed = (
        P(("depth", "col"), "row"),
        P(("depth", "row"), "col"),
        P(("depth", "row"), "col"),
        P(("depth", "row"), "col"),
        P("row", "col"),
        P("row", "col"),
    )
    return jax.shard_map(
        on_device,
        mesh=mesh,
        in_specs=placed,
        out_specs=(
            P(("depth", "col"), "row"),
            P(("row", "depth"), "col"),
            P(("row", "depth"), "col"),
        ),
        check_vma=False,
    )
```

```python
import jax
import jax.numpy as jnp
from jax import lax
from jax.experimental import pallas as pl
from jax.experimental.pallas import tpu as pltpu
from jax.sharding import PartitionSpec as P

NX, NY, NZ, NC = 4, 4, 8, 2
ROWS = 48
ZB = NX * ROWS
LAYER = NZ * ZB
UNITS = 3696
XB = 1920
WIDE = 128
DB = NX * WIDE
TB = 2 * ZB
HALF = WIDE // 2
CHUNKS = (640, 640, 640)
STARTS = (0, 640, 1280)
N_COPIES = 104
BF, F32 = jnp.bfloat16, jnp.float32

PIECES = (
    (0, 0, 0, 0, 1920),
    (0, 1920, 1, 0, 1776),
    (1, 0, 1, 1792, 128),
    (1, 128, 2, 0, 1920),
    (1, 2048, 3, 0, 1648),
)
PADS = ((1, 1664, 1792), (3, 1536, 1920))


def kernel(
    x_ref, gate_ref, up_ref, grad_ref, gw_ref, uw_ref,
    ig_ref, go_ref, uo_ref,
    own_g, g0, g1, g2, own_w, w_all, xt_own, xt, part, part_in, summed, summed_in,
    wp0, wp1, wp2, wr0, wr1, wr2, ws0, ws1, ws2, w_out,
    send_sem, recv_sem, local_sem,
):
    row, y, c = lax.axis_index("row"), lax.axis_index("col"), lax.axis_index("depth")
    z, x = row // NX, lax.rem(row, NX)
    g, wp, wr, ws = (g0, g1, g2), (wp0, wp1, wp2), (wr0, wr1, wr2), (ws0, ws1, ws2)
    last = len(CHUNKS) - 1

    def at(x_=x, y_=y, z_=z, c_=c):
        return (z_ * NX + x_, y_, c_)

    def turn(value, by, n):
        return lax.rem(value + (by + n), n)

    sends, locals_ = [], []

    def send(src, dst, device):
        i = len(sends)
        copy = pltpu.make_async_remote_copy(
            src_ref=src, dst_ref=dst, send_sem=send_sem.at[i], recv_sem=recv_sem.at[i],
            device_id=device, device_id_type=pl.DeviceIdType.MESH,
        )
        copy.start()
        sends.append(copy)
        return copy

    def local(src, dst):
        copy = pltpu.make_async_copy(src, dst, local_sem.at[len(locals_)])
        copy.start()
        locals_.append(copy)
        return copy

    partners = [at(x_=turn(x, o, NX)) for o in (1, 2, 3)]
    partners += [at(y_=turn(y, o, NY)) for o in (1, 2, 3)]
    partners += [at(z_=turn(z, o, NZ)) for o in (1, -1)]
    partners += [at(c_=1 - c)]
    barrier = pltpu.get_barrier_semaphore()
    for device in partners:
        pl.semaphore_signal(barrier, inc=1, device_id=device, device_id_type=pl.DeviceIdType.MESH)

    for block, first, end in PADS:
        own_g[block, :, first:end] = jnp.zeros((ROWS, end - first), BF)
    for which, first, block, there, columns in PIECES:
        for lo in range(0, columns, WIDE):
            n = min(WIDE, columns - lo)
            cut = slice(first + lo, first + lo + n)
            gate = gate_ref[:, cut].astype(F32)
            grad = grad_ref[:, cut].astype(F32)
            sigma = 1.0 / (1.0 + jnp.exp(-gate))
            if which == 0:
                value = grad * up_ref[:, cut].astype(F32) * sigma * (1.0 + gate * (1.0 - sigma))
            else:
                value = grad * gate * sigma
            own_g[block, :, there + lo:there + lo + n] = value.astype(BF)
    xt_own[...] = x_ref[...].astype(F32).T.astype(BF)

    pl.semaphore_wait(barrier, len(partners))

    mine = pl.ds(pl.multiple_of(row * ROWS, 16), ROWS)
    swapped = []

    def swap(k):
        cols = pl.ds(STARTS[k], CHUNKS[k])
        copies = []
        for o in (1, 2, 3):
            to = turn(x, o, NX)
            copies.append(send(own_g.at[to, :, cols], g[k].at[mine], at(x_=to)))
        swapped.append((copies, local(own_g.at[x, :, cols], g[k].at[mine])))

    swap(0)
    xt_rows = pl.ds(pl.multiple_of(x * WIDE, WIDE), WIDE)
    xt_cols = pl.ds(pl.multiple_of(y * TB, 128), TB)
    xt_x = [send(xt_own, xt.at[xt_rows, xt_cols], at(x_=turn(x, o, NX))) for o in (1, 2, 3)]
    xt_local = local(xt_own, xt.at[xt_rows, xt_cols])
    swap(1)

    for block, first, end in PADS:
        own_w[block, :, first:end] = jnp.zeros((WIDE, end - first), BF)
    for which, first, block, there, columns in PIECES:
        source = (gw_ref, uw_ref)[which]
        own_w[block, :, there:there + columns] = source[:, first:first + columns]

    def arrived(k):
        copies, copy = swapped[k]
        for remote in copies:
            remote.wait_recv()
        copy.wait()

    ring = {
        1: [(1, 0), (1, 1), (2, 0), (2, 1), (3, 0), (3, 1), (4, 0)],
        -1: [(1, 1), (1, 0), (2, 1), (2, 0), (3, 1), (3, 0), (4, 1)],
    }
    events = len(ring[1])
    moved = {(k, way): [] for k in range(len(CHUNKS)) for way in (1, -1)}

    def pass_on(k, e, way):
        if e >= events:
            k, e = k + 1, e - events
        if k > last:
            return
        hop, half = ring[way][e]
        block = turn(z, -way * (hop - 1), NZ)
        rows = pl.ds(pl.multiple_of(block * ZB + half * (ZB // 2), 16), ZB // 2)
        moved[k, way].append(send(g[k].at[rows], g[k].at[rows], at(z_=turn(z, way, NZ))))

    arrived(0)
    for e in (0, 1):
        for way in (1, -1):
            pass_on(0, e, way)
    swap(2)
    w_rows = pl.ds(pl.multiple_of(x * WIDE, WIDE), WIDE)
    w_sent = [
        send(own_w.at[turn(x, o, NX)], w_all.at[w_rows], at(x_=turn(x, o, NX))) for o in (1, 2, 3)
    ]
    w_local = local(own_w.at[x], w_all.at[w_rows])
    for copy in xt_x:
        copy.wait_recv()
    xt_local.wait()
    xt_y = [send(xt.at[:, xt_cols], xt.at[:, xt_cols], at(y_=turn(y, o, NY))) for o in (1, 2, 3)]

    def weight_piece(k, lo):
        n = min(256, CHUNKS[k] - lo)
        value = jnp.dot(xt[...], g[k][:, lo:lo + n], preferred_element_type=F32).astype(BF)
        for b in range(NX):
            for h in range(NC):
                wp[k][h, b * HALF:(b + 1) * HALF, lo:lo + n] = value[
                    b * WIDE + h * HALF:b * WIDE + (h + 1) * HALF
                ]

    exchanged = {}

    def exchange(k):
        exchanged[k] = send(wp[k].at[1 - c], wr[k], at(c_=1 - c))

    returned = []

    def give_back(k):
        exchanged[k].wait_recv()
        ws[k][...] = (wp[k][c].astype(F32) + wr[k][...].astype(F32)).astype(BF)
        cols = pl.ds(STARTS[k], CHUNKS[k])

        def rows(of):
            return pl.ds(pl.multiple_of(of * HALF, HALF), HALF)

        for o in (1, 2, 3):
            to = turn(x, o, NX)
            returned.append(send(ws[k].at[rows(to)], w_out.at[x, :, cols], at(x_=to)).wait_recv)
        returned.append(local(ws[k].at[rows(x)], w_out.at[x, :, cols]).wait)

    partial = {}

    def rows_of(b):
        return pl.ds(pl.multiple_of(turn(z, b, NZ) * ZB, 64), ZB)

    def input_part(b):
        rows = rows_of(b)
        total = None
        for k in range(len(CHUNKS)):
            term = lax.dot_general(
                g[k][rows, :], w_all[:, STARTS[k]:STARTS[k] + CHUNKS[k]],
                (((1,), (1,)), ((), ())), preferred_element_type=F32,
            )
            total = term if total is None else total + term
        for b_ in range(NX):
            part[b_, rows, :] = total[:, b_ * WIDE:(b_ + 1) * WIDE].astype(BF)
        partial[b] = [
            send(part.at[turn(x, o, NX), rows], part_in.at[o - 1, rows], at(x_=turn(x, o, NX)))
            for o in (1, 2, 3)
        ]

    def input_sum(b):
        rows = rows_of(b)
        for copy in partial[b]:
            copy.wait_recv()
        total = part[x, rows, :].astype(F32)
        for o in range(3):
            total = total + part_in[o, rows, :].astype(F32)
        summed[rows, :] = total.astype(BF)

    for k in range(len(CHUNKS)):
        for e in range(events):
            if e == events - 2 and k < last:
                arrived(k + 1)
            for way in (1, -1):
                moved[k, way][e].wait_recv()
                pass_on(k, e + 2, way)
            if k == 1 and e == 0:
                for copy in xt_y:
                    copy.wait_recv()
            if k >= 1:
                if e * 256 < CHUNKS[k - 1]:
                    weight_piece(k - 1, e * 256)
                if e == 3:
                    exchange(k - 1)
                if e == 5:
                    give_back(k - 1)
            if k == last:
                if e == 0:
                    for copy in w_sent:
                        copy.wait_recv()
                    w_local.wait()
                for b in ((0,), (-1,), (1,), (-2,), (2,), (-3, 3), (4,))[e]:
                    input_part(b)
                for b in ((), (), (0,), (-1,), (1,), (-2,), (2,))[e]:
                    input_sum(b)

    for lo in range(0, CHUNKS[last], 256):
        weight_piece(last, lo)
    exchange(last)
    for b in (-3, 3, 4):
        input_sum(b)

    def tokens(of):
        return pl.ds(pl.multiple_of(of * TB, 128), TB)

    over_y = [
        send(summed.at[tokens(turn(y, o, NY))], summed_in.at[o - 1], at(y_=turn(y, o, NY)))
        for o in (1, 2, 3)
    ]
    give_back(last)
    for copy in over_y:
        copy.wait_recv()
    total = summed[tokens(y), :].astype(F32)
    for o in range(3):
        total = total + summed_in[o].astype(F32)
    ig_ref[...] = total.astype(BF)

    for wait in returned:
        wait()
    for which, first, block, there, columns in PIECES:
        target = (go_ref, uo_ref)[which]
        target[:, first:first + columns] = w_out[block, :, there:there + columns]
    for copy in sends:
        copy.wait_send()


def on_device(layer_input, gate_pre, up_pre, hidden_grad, gate_weight, up_weight):
    vmem = pltpu.VMEM
    scratch = [vmem((NX, ROWS, XB), BF)]
    scratch += [vmem((LAYER, w), BF) for w in CHUNKS]
    scratch += [
        vmem((NX, WIDE, XB), BF),
        vmem((DB, XB), BF),
        vmem((WIDE, TB), BF),
        vmem((DB, LAYER), BF),
        vmem((NX, LAYER, WIDE), BF),
        vmem((NX - 1, LAYER, WIDE), BF),
        vmem((LAYER, WIDE), BF),
        vmem((NY - 1, TB, WIDE), BF),
    ]
    scratch += [vmem((NC, NX * HALF, w), BF) for w in CHUNKS]
    scratch += [vmem((NX * HALF, w), BF) for w in CHUNKS]
    scratch += [vmem((NX * HALF, w), BF) for w in CHUNKS]
    scratch += [vmem((NX, HALF, XB), BF)]
    scratch += [
        pltpu.SemaphoreType.DMA((N_COPIES,)),
        pltpu.SemaphoreType.DMA((N_COPIES,)),
        pltpu.SemaphoreType.DMA((8,)),
    ]
    in_vmem = pl.BlockSpec(memory_space=pltpu.VMEM)
    return pl.pallas_call(
        kernel,
        out_shape=(
            jax.ShapeDtypeStruct((TB, WIDE), BF),
            jax.ShapeDtypeStruct((HALF, UNITS), BF),
            jax.ShapeDtypeStruct((HALF, UNITS), BF),
        ),
        in_specs=[in_vmem] * 6,
        out_specs=(in_vmem,) * 3,
        scratch_shapes=scratch,
        compiler_params=pltpu.CompilerParams(
            collective_id=0, has_side_effects=True, vmem_limit_bytes=56 * 1024 * 1024
        ),
    )(layer_input, gate_pre, up_pre, hidden_grad, gate_weight, up_weight)


def solution(mesh):
    placed = (
        P(("depth", "col"), "row"),
        P(("depth", "row"), "col"),
        P(("depth", "row"), "col"),
        P(("depth", "row"), "col"),
        P("row", "col"),
        P("row", "col"),
    )
    return jax.shard_map(
        on_device,
        mesh=mesh,
        in_specs=placed,
        out_specs=(
            P(("depth", "col"), "row"),
            P(("row", "depth"), "col"),
            P(("row", "depth"), "col"),
        ),
        check_vma=False,
    )
```

```python
import jax
import jax.numpy as jnp
from jax import lax
from jax.experimental import pallas as pl
from jax.experimental.pallas import tpu as pltpu
from jax.sharding import PartitionSpec as P

NX, NY, NZ, NC = 4, 4, 8, 2
ROWS = 48
ZB = NX * ROWS
LAYER = NZ * ZB
UNITS = 3696
XB = 1920
TILES = 29
WIDE = 128
DB = NX * WIDE
TB = 2 * ZB
HALF = WIDE // 2
CHUNKS = (640, 640, 640)
STARTS = (0, 640, 1280)
N_COPIES = 112
BF, F32 = jnp.bfloat16, jnp.float32

PIECES = (
    (0, 0, 0, 0, 1920),
    (0, 1920, 1, 0, 1776),
    (1, 0, 1, 1792, 128),
    (1, 128, 2, 0, 1920),
    (1, 2048, 3, 0, 1648),
)
PADS = ((1, 1664, 1792), (3, 1536, 1920))
ROW_PADS = ((1, 1776, 1792), (3, 1648, 1920))


def kernel(
    x_hbm, gate_hbm, up_hbm, grad_hbm, gw_hbm, uw_hbm,
    ig_ref, w_out,
    x_ref, gate_ref, up_ref, grad_ref, own_g, g0, g1, g2, own_w, w_all, xt_own, xt, part, part_in, summed, summed_in,
    wp0, wp1, wp2, wr0, wr1, wr2, ws0, ws1, ws2,
    send_sem, recv_sem, local_sem, y_send, y_recv,
):
    row, y, c = lax.axis_index("row"), lax.axis_index("col"), lax.axis_index("depth")
    z, x = row // NX, lax.rem(row, NX)
    g, wp, wr, ws = (g0, g1, g2), (wp0, wp1, wp2), (wr0, wr1, wr2), (ws0, ws1, ws2)
    last = len(CHUNKS) - 1

    def at(x_=x, y_=y, z_=z, c_=c):
        return (z_ * NX + x_, y_, c_)

    def turn(value, by, n):
        return lax.rem(value + (by + n), n)

    sends, locals_ = [], []

    def send(src, dst, device):
        i = len(sends)
        copy = pltpu.make_async_remote_copy(
            src_ref=src, dst_ref=dst, send_sem=send_sem.at[i], recv_sem=recv_sem.at[i],
            device_id=device, device_id_type=pl.DeviceIdType.MESH,
        )
        copy.start()
        sends.append(copy)
        return copy

    def local(src, dst):
        copy = pltpu.make_async_copy(src, dst, local_sem.at[len(locals_)])
        copy.start()
        locals_.append(copy)
        return copy

    partners = [at(x_=turn(x, o, NX)) for o in (1, 2, 3)]
    partners += [at(y_=turn(y, o, NY)) for o in (1, 2, 3)]
    partners += [at(z_=turn(z, o, NZ)) for o in (1, -1)]
    partners += [at(c_=1 - c)]
    barrier = pltpu.get_barrier_semaphore()
    for device in partners:
        pl.semaphore_signal(barrier, inc=1, device_id=device, device_id_type=pl.DeviceIdType.MESH)

    loads = [
        local(src, dst)
        for src, dst in ((gate_hbm, gate_ref), (up_hbm, up_ref), (grad_hbm, grad_ref), (x_hbm, x_ref))
    ]
    w_loads = [
        local(
            (gw_hbm, uw_hbm)[which].at[pl.ds(first, columns)],
            own_w.at[block, pl.ds(there, columns)],
        )
        for which, first, block, there, columns in PIECES
    ]
    for block, first, end in ROW_PADS:
        own_w[block, first:end, :] = jnp.zeros((end - first, WIDE), BF)
    for block, first, end in PADS:
        own_g[block, :, first:end] = jnp.zeros((ROWS, end - first), BF)
    for load in loads[:3]:
        load.wait()

    done = set()

    def gated(k):
        for t in range(TILES):
            chunks = [(tile % (XB // WIDE)) * WIDE // CHUNKS[0] for tile in (t, TILES + t)]
            if k not in chunks or t in done:
                continue
            done.add(t)
            n = min(WIDE, UNITS - t * WIDE)
            cut = slice(t * WIDE, t * WIDE + n)
            gate = gate_ref[:, cut].astype(F32)
            grad = grad_ref[:, cut].astype(F32)
            sigma = 1.0 / (1.0 + jnp.exp(-gate))
            scaled = grad * sigma
            values = (
                scaled * up_ref[:, cut].astype(F32) * (1.0 + gate * (1.0 - sigma)), scaled * gate
            )
            for tile, value in zip((t, TILES + t), values):
                block, first = divmod(tile * WIDE, XB)
                own_g[block, :, first:first + n] = value.astype(BF)

    gated(0)
    pl.semaphore_wait(barrier, len(partners))

    def slab(of):
        return pl.ds(pl.multiple_of((z * NX + of) * ROWS, 16), ROWS)

    mates = {1: x + 1 - 2 * lax.rem(x, 2), 2: turn(x, 2, NX), 3: 3 - x}
    swapped, first_hop = [], {}

    def swap(k):
        cols = pl.ds(STARTS[k], CHUNKS[k])
        for way in (1, -1):
            first_hop[k, way] = send(
                own_g.at[x, :, cols], g[k].at[slab(x)], at(z_=turn(z, way, NZ))
            )
        copies = {}
        for m in (1, 3, 2):
            copies[m] = send(own_g.at[mates[m], :, cols], g[k].at[slab(x)], at(x_=mates[m]))
        swapped.append((copies, local(own_g.at[x, :, cols], g[k].at[slab(x)])))

    def arrived(k):
        copies, copy = swapped[k]
        for m in (1, 2, 3):
            copies[m].wait_recv()
        copy.wait()

    near, far = [(h, s) for h in (1, 2, 3) for s in (0, 1)], [(h, s) for h in (1, 2, 3) for s in (1, 0)]
    items = {1: [], -1: [(0, h, s) for h, s in near]}
    for k in range(len(CHUNKS)):
        items[1] += [(k, h, s) for h, s in near + [(4, 0)]]
        if k:
            items[-1] += [(k, h, s) for h, s in far + [(4, 1)]]
    items[-1].insert(7, (0, 4, 1))
    events = 7
    moved = {1: [], -1: []}

    def pass_on(i, way):
        if i >= len(items[way]):
            return
        k, hop, half = items[way][i]
        to = at(z_=turn(z, way, NZ))
        if (hop, half) == (1, 0):
            rows = slab(mates[1])
            moved[way].append((first_hop[k, way], send(g[k].at[rows], g[k].at[rows], to)))
            return
        block = turn(z, -way * (hop - 1), NZ)
        part_ = x // 2 if half == 0 else 1 - x // 2
        rows = pl.ds(pl.multiple_of(block * ZB + part_ * (ZB // 2), 16), ZB // 2)
        moved[way].append((send(g[k].at[rows], g[k].at[rows], to),))

    swap(0)
    gated(1)
    swap(1)
    swapped[0][0][1].wait_recv()
    for way in (1, -1):
        pass_on(0, way)
    gated(2)
    swap(2)
    for m in (2, 3):
        swapped[0][0][m].wait_recv()
    swapped[0][1].wait()
    for way in (1, -1):
        pass_on(1, way)
    loads[3].wait()
    xt_own[...] = x_ref[...].astype(F32).T.astype(BF)
    xt_rows = pl.ds(pl.multiple_of(x * WIDE, WIDE), WIDE)
    xt_cols = pl.ds(pl.multiple_of(y * TB, 128), TB)
    xt_x = [send(xt_own, xt.at[xt_rows, xt_cols], at(x_=turn(x, o, NX))) for o in (1, 2, 3)]
    xt_local = local(xt_own, xt.at[xt_rows, xt_cols])
    for load in w_loads:
        load.wait()

    w_half = pl.ds(pl.multiple_of(c * (XB // 2), 64), XB // 2)
    w_cols = pl.ds(pl.multiple_of(x * WIDE, WIDE), WIDE)
    w_sent = [
        send(
            own_w.at[turn(x, o, NX), w_half], w_all.at[w_half, w_cols], at(x_=turn(x, o, NX))
        )
        for o in (1, 2, 3)
    ]
    w_local = local(own_w.at[x, w_half], w_all.at[w_half, w_cols])
    for copy in xt_x:
        copy.wait_recv()
    xt_local.wait()
    xt_y = [send(xt.at[:, xt_cols], xt.at[:, xt_cols], at(y_=turn(y, o, NY))) for o in (1, 2, 3)]

    def weight_piece(k, lo):
        n = min(256, CHUNKS[k] - lo)
        value = jnp.dot(xt[...], g[k][:, lo:lo + n], preferred_element_type=F32).astype(BF)
        for b in range(NX):
            for h in range(NC):
                wp[k][h, b * HALF:(b + 1) * HALF, lo:lo + n] = value[
                    b * WIDE + h * HALF:b * WIDE + (h + 1) * HALF
                ]

    exchanged = {}

    def exchange(k):
        exchanged[k] = send(wp[k].at[1 - c], wr[k], at(c_=1 - c))

    returned = []

    def give_back(k):
        exchanged[k].wait_recv()
        ws[k][...] = (wp[k][c].astype(F32) + wr[k][...].astype(F32)).astype(BF)
        cols = pl.ds(STARTS[k], CHUNKS[k])

        def rows(of):
            return pl.ds(pl.multiple_of(of * HALF, HALF), HALF)

        for o in (1, 2, 3):
            to = turn(x, o, NX)
            returned.append(send(ws[k].at[rows(to)], w_out.at[x, :, cols], at(x_=to)).wait_recv)
        returned.append(local(ws[k].at[rows(x)], w_out.at[x, :, cols]).wait)

    partial, scattered = {}, []

    def rows_of(b):
        return pl.ds(pl.multiple_of(turn(z, b, NZ) * ZB, 64), ZB)

    def input_part(b):
        rows = rows_of(b)
        total = None
        for k in range(len(CHUNKS)):
            term = jnp.dot(
                g[k][rows, :], w_all[STARTS[k]:STARTS[k] + CHUNKS[k], :],
                preferred_element_type=F32,
            )
            total = term if total is None else total + term
        for b_ in range(NX):
            part[b_, rows, :] = total[:, b_ * WIDE:(b_ + 1) * WIDE].astype(BF)
        partial[b] = [
            send(part.at[turn(x, o, NX), rows], part_in.at[o - 1, rows], at(x_=turn(x, o, NX)))
            for o in (1, 2, 3)
        ]

    def input_sum(b):
        rows = rows_of(b)
        for copy in partial[b]:
            copy.wait_recv()
        total = part[x, rows, :].astype(F32)
        for o in range(3):
            total = total + part_in[o, rows, :].astype(F32)
        summed[rows, :] = total.astype(BF)
        block = turn(z, b, NZ)
        owner, parity = block // 2, lax.rem(block, 2)
        away = turn(owner - y, 0, NY)
        copy = pltpu.make_async_remote_copy(
            src_ref=summed.at[rows],
            dst_ref=summed_in.at[lax.rem(away + 3, NY), pl.ds(pl.multiple_of(parity * ZB, 64), ZB)],
            send_sem=y_send.at[b + 3], recv_sem=y_recv.at[2 * away + parity],
            device_id=at(y_=owner), device_id_type=pl.DeviceIdType.MESH,
        )
        scattered.append((away, copy))

        @pl.when(away != 0)
        def _():
            copy.start()

    over_core = []
    parts_at = {(1, 6): (0,), (2, 1): (-1, 1), (2, 3): (-2, 2), (2, 5): (-3, 3), (2, 6): (4,)}
    sums_at = {(2, 1): (0,), (2, 4): (-1, 1), (2, 6): (-2, 2)}
    for k in range(len(CHUNKS)):
        for e in range(events):
            if e == 4 and k < last:
                arrived(k + 1)
            for way in (1, -1):
                for copy in moved[way][k * events + e]:
                    copy.wait_recv()
                pass_on(k * events + e + 2, way)
            if (k, e) == (1, 0):
                for copy in xt_y:
                    copy.wait_recv()
            if (k, e) == (1, 4):
                for copy in w_sent:
                    copy.wait_recv()
                w_local.wait()
                over_core.append(send(w_all.at[w_half], w_all.at[w_half], at(c_=1 - c)))
            if (k, e) == (1, 6):
                over_core[0].wait_recv()
            for b in parts_at.get((k, e), ()):
                input_part(b)
            if k >= 1:
                if e < 3 and e * 256 < CHUNKS[k - 1]:
                    weight_piece(k - 1, e * 256)
                if e == 2:
                    exchange(k - 1)
                if e == 4:
                    give_back(k - 1)
            for b in sums_at.get((k, e), ()):
                input_sum(b)

    for lo in range(0, CHUNKS[last], 256):
        weight_piece(last, lo)
    exchange(last)
    for b in (-3, 3, 4):
        input_sum(b)
    give_back(last)

    for o in (1, 2, 3):
        for parity in (0, 1):
            landed = summed_in.at[o - 1, pl.ds(parity * ZB, ZB)]
            pltpu.make_async_remote_copy(
                src_ref=landed, dst_ref=landed,
                send_sem=y_send.at[0], recv_sem=y_recv.at[2 * o + parity],
                device_id=at(y_=turn(y, o, NY)), device_id_type=pl.DeviceIdType.MESH,
            ).wait_recv()
    total = summed[pl.ds(pl.multiple_of(y * TB, 128), TB), :].astype(F32)
    for o in range(3):
        total = total + summed_in[o].astype(F32)
    ig_ref[...] = total.astype(BF)

    for wait in returned:
        wait()
    for copy in sends:
        copy.wait_send()
    for away, copy in scattered:
        pl.when(away != 0)(copy.wait_send)


def unpack(ig_in, w_out, ig_ref, go_ref, uo_ref):
    ig_ref[...] = ig_in[...]
    for which, first, block, there, columns in PIECES:
        target = (go_ref, uo_ref)[which]
        target[:, first:first + columns] = w_out[block, :, there:there + columns]


def on_device(layer_input, gate_pre, up_pre, hidden_grad, gate_weight, up_weight):
    vmem = pltpu.VMEM
    scratch = [vmem((TB, WIDE), BF)] + [vmem((ROWS, UNITS), BF)] * 3 + [vmem((NX, ROWS, XB), BF)]
    scratch += [vmem((LAYER, w), BF) for w in CHUNKS]
    scratch += [
        vmem((NX, XB, WIDE), BF),
        vmem((XB, DB), BF),
        vmem((WIDE, TB), BF),
        vmem((DB, LAYER), BF),
        vmem((NX, LAYER, WIDE), BF),
        vmem((NX - 1, LAYER, WIDE), BF),
        vmem((LAYER, WIDE), BF),
        vmem((NY, TB, WIDE), BF),
    ]
    scratch += [vmem((NC, NX * HALF, w), BF) for w in CHUNKS]
    scratch += [vmem((NX * HALF, w), BF) for w in CHUNKS]
    scratch += [vmem((NX * HALF, w), BF) for w in CHUNKS]
    scratch += [
        pltpu.SemaphoreType.DMA((N_COPIES,)),
        pltpu.SemaphoreType.DMA((N_COPIES,)),
        pltpu.SemaphoreType.DMA((20,)),
        pltpu.SemaphoreType.DMA((NZ,)),
        pltpu.SemaphoreType.DMA((2 * NY,)),
    ]
    in_vmem = pl.BlockSpec(memory_space=pltpu.VMEM)
    anywhere = pl.BlockSpec(memory_space=pl.ANY)
    input_grad, packed = pl.pallas_call(
        kernel,
        out_shape=(
            jax.ShapeDtypeStruct((TB, WIDE), BF),
            jax.ShapeDtypeStruct((NX, HALF, XB), BF),
        ),
        in_specs=[anywhere] * 6,
        out_specs=(in_vmem, anywhere),
        scratch_shapes=scratch,
        compiler_params=pltpu.CompilerParams(
            collective_id=0, has_side_effects=True, vmem_limit_bytes=56 * 1024 * 1024
        ),
    )(layer_input, gate_pre, up_pre, hidden_grad, gate_weight.T, up_weight.T)
    return pl.pallas_call(
        unpack,
        out_shape=(
            jax.ShapeDtypeStruct((TB, WIDE), BF),
            jax.ShapeDtypeStruct((HALF, UNITS), BF),
            jax.ShapeDtypeStruct((HALF, UNITS), BF),
        ),
        in_specs=[in_vmem] * 2,
        out_specs=(in_vmem,) * 3,
    )(input_grad, packed)


def solution(mesh):
    placed = (
        P(("depth", "col"), "row"),
        P(("depth", "row"), "col"),
        P(("depth", "row"), "col"),
        P(("depth", "row"), "col"),
        P("row", "col"),
        P("row", "col"),
    )
    return jax.shard_map(
        on_device,
        mesh=mesh,
        in_specs=placed,
        out_specs=(
            P(("depth", "col"), "row"),
            P(("row", "depth"), "col"),
            P(("row", "depth"), "col"),
        ),
        check_vma=False,
    )
```

```python
import jax
import jax.numpy as jnp
from jax import lax
from jax.experimental import pallas as pl
from jax.experimental.pallas import tpu as pltpu
from jax.sharding import PartitionSpec as P

NX, NY, NZ, NC = 4, 4, 8, 2
ROWS = 48
ZB = NX * ROWS
LAYER = NZ * ZB
UNITS = 3696
XB = 1920
TILES = 29
WIDE = 128
DB = NX * WIDE
TB = 2 * ZB
HALF = WIDE // 2
CHUNKS = (640, 640, 640)
STARTS = (0, 640, 1280)
N_COPIES = 112
BF, F32 = jnp.bfloat16, jnp.float32

PIECES = (
    (0, 0, 0, 0, 1920),
    (0, 1920, 1, 0, 1776),
    (1, 0, 1, 1792, 128),
    (1, 128, 2, 0, 1920),
    (1, 2048, 3, 0, 1648),
)
PADS = ((1, 1664, 1792), (3, 1536, 1920))
ROW_PADS = ((1, 1776, 1792), (3, 1648, 1920))


def kernel(
    x_hbm, gate_hbm, up_hbm, grad_hbm, gw_hbm, uw_hbm,
    ig_ref, w_out,
    x_ref, gate_ref, up_ref, grad_ref, own_g, g0, g1, g2, own_w, w_all, xt_own, xt, part, part_in, summed, summed_in,
    wp0, wp1, wp2, wr0, wr1, wr2, ws0, ws1, ws2,
    send_sem, recv_sem, local_sem, y_send, y_recv,
):
    row, y, c = lax.axis_index("row"), lax.axis_index("col"), lax.axis_index("depth")
    z, x = row // NX, lax.rem(row, NX)
    g, wp, wr, ws = (g0, g1, g2), (wp0, wp1, wp2), (wr0, wr1, wr2), (ws0, ws1, ws2)
    last = len(CHUNKS) - 1

    def at(x_=x, y_=y, z_=z, c_=c):
        return (z_ * NX + x_, y_, c_)

    def turn(value, by, n):
        return lax.rem(value + (by + n), n)

    sends, locals_ = [], []

    def send(src, dst, device):
        i = len(sends)
        copy = pltpu.make_async_remote_copy(
            src_ref=src, dst_ref=dst, send_sem=send_sem.at[i], recv_sem=recv_sem.at[i],
            device_id=device, device_id_type=pl.DeviceIdType.MESH,
        )
        copy.start()
        sends.append(copy)
        return copy

    def local(src, dst):
        copy = pltpu.make_async_copy(src, dst, local_sem.at[len(locals_)])
        copy.start()
        locals_.append(copy)
        return copy

    partners = [at(x_=turn(x, o, NX)) for o in (1, 2, 3)]
    partners += [at(y_=turn(y, o, NY)) for o in (1, 2, 3)]
    partners += [at(z_=turn(z, o, NZ)) for o in (1, -1)]
    partners += [at(c_=1 - c)]
    barrier = pltpu.get_barrier_semaphore()
    for device in partners:
        pl.semaphore_signal(barrier, inc=1, device_id=device, device_id_type=pl.DeviceIdType.MESH)

    loads = [
        local(src, dst)
        for src, dst in ((gate_hbm, gate_ref), (up_hbm, up_ref), (grad_hbm, grad_ref), (x_hbm, x_ref))
    ]
    w_loads = [
        local(
            (gw_hbm, uw_hbm)[which].at[pl.ds(first, columns)],
            own_w.at[block, pl.ds(there, columns)],
        )
        for which, first, block, there, columns in PIECES
    ]
    for block, first, end in ROW_PADS:
        own_w[block, first:end, :] = jnp.zeros((end - first, WIDE), BF)
    for block, first, end in PADS:
        own_g[block, :, first:end] = jnp.zeros((ROWS, end - first), BF)
    for load in loads[:3]:
        load.wait()

    done = set()

    def gated(k):
        for t in range(TILES):
            chunks = [(tile % (XB // WIDE)) * WIDE // CHUNKS[0] for tile in (t, TILES + t)]
            if k not in chunks or t in done:
                continue
            done.add(t)
            n = min(WIDE, UNITS - t * WIDE)
            cut = slice(t * WIDE, t * WIDE + n)
            gate = gate_ref[:, cut].astype(F32)
            grad = grad_ref[:, cut].astype(F32)
            sigma = 1.0 / (1.0 + jnp.exp(-gate))
            scaled = grad * sigma
            values = (
                scaled * up_ref[:, cut].astype(F32) * (1.0 + gate * (1.0 - sigma)), scaled * gate
            )
            for tile, value in zip((t, TILES + t), values):
                block, first = divmod(tile * WIDE, XB)
                own_g[block, :, first:first + n] = value.astype(BF)

    gated(0)
    pl.semaphore_wait(barrier, len(partners))

    def slab(of):
        return pl.ds(pl.multiple_of((z * NX + of) * ROWS, 16), ROWS)

    mates = {1: x + 1 - 2 * lax.rem(x, 2), 2: turn(x, 2, NX), 3: 3 - x}
    swapped, first_hop = [], {}

    def swap(k):
        cols = pl.ds(STARTS[k], CHUNKS[k])
        for way in (1, -1):
            first_hop[k, way] = send(
                own_g.at[x, :, cols], g[k].at[slab(x)], at(z_=turn(z, way, NZ))
            )
        copies = {}
        for m in (1, 3, 2):
            copies[m] = send(own_g.at[mates[m], :, cols], g[k].at[slab(x)], at(x_=mates[m]))
        swapped.append((copies, local(own_g.at[x, :, cols], g[k].at[slab(x)])))

    def arrived(k):
        copies, copy = swapped[k]
        for m in (1, 2, 3):
            copies[m].wait_recv()
        copy.wait()

    near, far = [(h, s) for h in (1, 2, 3) for s in (0, 1)], [(h, s) for h in (1, 2, 3) for s in (1, 0)]
    items = {1: [], -1: [(0, h, s) for h, s in near]}
    for k in range(len(CHUNKS)):
        items[1] += [(k, h, s) for h, s in near + [(4, 0)]]
        if k:
            items[-1] += [(k, h, s) for h, s in far + [(4, 1)]]
    items[-1].insert(7, (0, 4, 1))
    events = 7
    moved = {1: [], -1: []}

    def pass_on(i, way):
        if i >= len(items[way]):
            return
        k, hop, half = items[way][i]
        to = at(z_=turn(z, way, NZ))
        if (hop, half) == (1, 0):
            rows = slab(mates[1])
            moved[way].append((first_hop[k, way], send(g[k].at[rows], g[k].at[rows], to)))
            return
        block = turn(z, -way * (hop - 1), NZ)
        part_ = x // 2 if half == 0 else 1 - x // 2
        rows = pl.ds(pl.multiple_of(block * ZB + part_ * (ZB // 2), 16), ZB // 2)
        moved[way].append((send(g[k].at[rows], g[k].at[rows], to),))

    swap(0)
    loads[3].wait()
    xt_own[...] = x_ref[...].astype(F32).T.astype(BF)
    xt_rows = pl.ds(pl.multiple_of(x * WIDE, WIDE), WIDE)
    xt_cols = pl.ds(pl.multiple_of(y * TB, 128), TB)
    xt_x = [send(xt_own, xt.at[xt_rows, xt_cols], at(x_=turn(x, o, NX))) for o in (1, 2, 3)]
    xt_local = local(xt_own, xt.at[xt_rows, xt_cols])
    gated(1)
    swap(1)
    swapped[0][0][1].wait_recv()
    for way in (1, -1):
        pass_on(0, way)
    gated(2)
    for m in (2, 3):
        swapped[0][0][m].wait_recv()
    swapped[0][1].wait()
    for way in (1, -1):
        pass_on(1, way)
    for copy in xt_x:
        copy.wait_recv()
    xt_local.wait()
    xt_y = [send(xt.at[:, xt_cols], xt.at[:, xt_cols], at(y_=turn(y, o, NY))) for o in (1, 2, 3)]
    for load in w_loads:
        load.wait()

    w_half = pl.ds(pl.multiple_of(c * (XB // 2), 64), XB // 2)
    w_cols = pl.ds(pl.multiple_of(x * WIDE, WIDE), WIDE)
    w_sent = [
        send(
            own_w.at[turn(x, o, NX), w_half], w_all.at[w_half, w_cols], at(x_=turn(x, o, NX))
        )
        for o in (1, 2, 3)
    ]
    w_local = local(own_w.at[x, w_half], w_all.at[w_half, w_cols])
    swap(2)

    def weight_piece(k, lo):
        n = min(256, CHUNKS[k] - lo)
        value = jnp.dot(xt[...], g[k][:, lo:lo + n], preferred_element_type=F32).astype(BF)
        for b in range(NX):
            for h in range(NC):
                wp[k][h, b * HALF:(b + 1) * HALF, lo:lo + n] = value[
                    b * WIDE + h * HALF:b * WIDE + (h + 1) * HALF
                ]

    exchanged = {}

    def exchange(k):
        exchanged[k] = send(wp[k].at[1 - c], wr[k], at(c_=1 - c))

    returned = []

    def give_back(k):
        exchanged[k].wait_recv()
        ws[k][...] = (wp[k][c].astype(F32) + wr[k][...].astype(F32)).astype(BF)
        cols = pl.ds(STARTS[k], CHUNKS[k])

        def rows(of):
            return pl.ds(pl.multiple_of(of * HALF, HALF), HALF)

        for o in (1, 2, 3):
            to = turn(x, o, NX)
            returned.append(send(ws[k].at[rows(to)], w_out.at[x, :, cols], at(x_=to)).wait_recv)
        returned.append(local(ws[k].at[rows(x)], w_out.at[x, :, cols]).wait)

    partial, scattered = {}, []

    def rows_of(b):
        return pl.ds(pl.multiple_of(turn(z, b, NZ) * ZB, 64), ZB)

    def input_part(b):
        rows = rows_of(b)
        total = None
        for k in range(len(CHUNKS)):
            term = jnp.dot(
                g[k][rows, :], w_all[STARTS[k]:STARTS[k] + CHUNKS[k], :],
                preferred_element_type=F32,
            )
            total = term if total is None else total + term
        for b_ in range(NX):
            part[b_, rows, :] = total[:, b_ * WIDE:(b_ + 1) * WIDE].astype(BF)
        partial[b] = [
            send(part.at[turn(x, o, NX), rows], part_in.at[o - 1, rows], at(x_=turn(x, o, NX)))
            for o in (1, 2, 3)
        ]

    def input_sum(b):
        rows = rows_of(b)
        for copy in partial[b]:
            copy.wait_recv()
        total = part[x, rows, :].astype(F32)
        for o in range(3):
            total = total + part_in[o, rows, :].astype(F32)
        summed[rows, :] = total.astype(BF)
        block = turn(z, b, NZ)
        owner, parity = block // 2, lax.rem(block, 2)
        away = turn(owner - y, 0, NY)
        copy = pltpu.make_async_remote_copy(
            src_ref=summed.at[rows],
            dst_ref=summed_in.at[lax.rem(away + 3, NY), pl.ds(pl.multiple_of(parity * ZB, 64), ZB)],
            send_sem=y_send.at[b + 3], recv_sem=y_recv.at[2 * away + parity],
            device_id=at(y_=owner), device_id_type=pl.DeviceIdType.MESH,
        )
        scattered.append((away, copy))

        @pl.when(away != 0)
        def _():
            copy.start()

    over_core = []
    parts_at = {(1, 6): (0,), (2, 1): (-1, 1), (2, 3): (-2, 2), (2, 5): (-3, 3), (2, 6): (4,)}
    sums_at = {(2, 1): (0,), (2, 4): (-1, 1), (2, 6): (-2, 2)}
    for k in range(len(CHUNKS)):
        for e in range(events):
            if e == 4 and k < last:
                arrived(k + 1)
            for way in (1, -1):
                for copy in moved[way][k * events + e]:
                    copy.wait_recv()
                pass_on(k * events + e + 2, way)
            if (k, e) == (1, 2):
                for copy in xt_y:
                    copy.wait_recv()
            if (k, e) == (1, 4):
                for copy in w_sent:
                    copy.wait_recv()
                w_local.wait()
                over_core.append(send(w_all.at[w_half], w_all.at[w_half], at(c_=1 - c)))
            if (k, e) == (1, 6):
                over_core[0].wait_recv()
            for b in parts_at.get((k, e), ()):
                input_part(b)
            if k >= 1:
                piece = e - (2 if k == 1 else 0)
                if 0 <= piece < 3 and piece * 256 < CHUNKS[k - 1]:
                    weight_piece(k - 1, piece * 256)
                if piece == 2:
                    exchange(k - 1)
                if piece == (4 if k == 1 else 3):
                    give_back(k - 1)
            for b in sums_at.get((k, e), ()):
                input_sum(b)

    for lo in range(0, CHUNKS[last], 256):
        weight_piece(last, lo)
    exchange(last)
    for b in (-3, 3, 4):
        input_sum(b)
    give_back(last)

    for o in (1, 2, 3):
        for parity in (0, 1):
            landed = summed_in.at[o - 1, pl.ds(parity * ZB, ZB)]
            pltpu.make_async_remote_copy(
                src_ref=landed, dst_ref=landed,
                send_sem=y_send.at[0], recv_sem=y_recv.at[2 * o + parity],
                device_id=at(y_=turn(y, o, NY)), device_id_type=pl.DeviceIdType.MESH,
            ).wait_recv()
    total = summed[pl.ds(pl.multiple_of(y * TB, 128), TB), :].astype(F32)
    for o in range(3):
        total = total + summed_in[o].astype(F32)
    ig_ref[...] = total.astype(BF)

    for wait in returned:
        wait()
    for copy in sends:
        copy.wait_send()
    for away, copy in scattered:
        pl.when(away != 0)(copy.wait_send)


def unpack(ig_in, w_out, ig_ref, go_ref, uo_ref):
    ig_ref[...] = ig_in[...]
    for which, first, block, there, columns in PIECES:
        target = (go_ref, uo_ref)[which]
        target[:, first:first + columns] = w_out[block, :, there:there + columns]


def on_device(layer_input, gate_pre, up_pre, hidden_grad, gate_weight, up_weight):
    vmem = pltpu.VMEM
    scratch = [vmem((TB, WIDE), BF)] + [vmem((ROWS, UNITS), BF)] * 3 + [vmem((NX, ROWS, XB), BF)]
    scratch += [vmem((LAYER, w), BF) for w in CHUNKS]
    scratch += [
        vmem((NX, XB, WIDE), BF),
        vmem((XB, DB), BF),
        vmem((WIDE, TB), BF),
        vmem((DB, LAYER), BF),
        vmem((NX, LAYER, WIDE), BF),
        vmem((NX - 1, LAYER, WIDE), BF),
        vmem((LAYER, WIDE), BF),
        vmem((NY, TB, WIDE), BF),
    ]
    scratch += [vmem((NC, NX * HALF, w), BF) for w in CHUNKS]
    scratch += [vmem((NX * HALF, w), BF) for w in CHUNKS]
    scratch += [vmem((NX * HALF, w), BF) for w in CHUNKS]
    scratch += [
        pltpu.SemaphoreType.DMA((N_COPIES,)),
        pltpu.SemaphoreType.DMA((N_COPIES,)),
        pltpu.SemaphoreType.DMA((20,)),
        pltpu.SemaphoreType.DMA((NZ,)),
        pltpu.SemaphoreType.DMA((2 * NY,)),
    ]
    in_vmem = pl.BlockSpec(memory_space=pltpu.VMEM)
    anywhere = pl.BlockSpec(memory_space=pl.ANY)
    input_grad, packed = pl.pallas_call(
        kernel,
        out_shape=(
            jax.ShapeDtypeStruct((TB, WIDE), BF),
            jax.ShapeDtypeStruct((NX, HALF, XB), BF),
        ),
        in_specs=[anywhere] * 6,
        out_specs=(in_vmem, anywhere),
        scratch_shapes=scratch,
        compiler_params=pltpu.CompilerParams(
            collective_id=0, has_side_effects=True, vmem_limit_bytes=56 * 1024 * 1024
        ),
    )(layer_input, gate_pre, up_pre, hidden_grad, gate_weight.T, up_weight.T)
    return pl.pallas_call(
        unpack,
        out_shape=(
            jax.ShapeDtypeStruct((TB, WIDE), BF),
            jax.ShapeDtypeStruct((HALF, UNITS), BF),
            jax.ShapeDtypeStruct((HALF, UNITS), BF),
        ),
        in_specs=[in_vmem] * 2,
        out_specs=(in_vmem,) * 3,
    )(input_grad, packed)


def solution(mesh):
    placed = (
        P(("depth", "col"), "row"),
        P(("depth", "row"), "col"),
        P(("depth", "row"), "col"),
        P(("depth", "row"), "col"),
        P("row", "col"),
        P("row", "col"),
    )
    return jax.shard_map(
        on_device,
        mesh=mesh,
        in_specs=placed,
        out_specs=(
            P(("depth", "col"), "row"),
            P(("row", "depth"), "col"),
            P(("row", "depth"), "col"),
        ),
        check_vma=False,
    )
```

```python
import jax
import jax.numpy as jnp
from jax import lax
from jax.experimental import pallas as pl
from jax.experimental.pallas import tpu as pltpu
from jax.sharding import PartitionSpec as P

NX, NY, NZ, NC = 4, 4, 8, 2
ROWS = 48
ZB = NX * ROWS
LAYER = NZ * ZB
UNITS = 3696
XB = 1920
TILES = 29
WIDE = 128
DB = NX * WIDE
TB = 2 * ZB
HALF = WIDE // 2
CHUNKS = (640, 640, 640)
STARTS = (0, 640, 1280)
N_COPIES = 112
BF, F32 = jnp.bfloat16, jnp.float32

PIECES = (
    (0, 0, 0, 0, 1920),
    (0, 1920, 1, 0, 1776),
    (1, 0, 1, 1792, 128),
    (1, 128, 2, 0, 1920),
    (1, 2048, 3, 0, 1648),
)
PADS = ((1, 1664, 1792), (3, 1536, 1920))
ROW_PADS = ((1, 1776, 1792), (3, 1648, 1920))


def kernel(
    x_hbm, gate_hbm, up_hbm, grad_hbm, gw_hbm, uw_hbm,
    ig_ref, w_out,
    x_ref, gate_ref, up_ref, grad_ref, own_g, g0, g1, g2, own_w, w_all, xt_own, xt, part, part_in, summed, summed_in,
    wp0, wp1, wp2, wr0, wr1, wr2, ws0, ws1, ws2,
    send_sem, recv_sem, local_sem, y_send, y_recv,
):
    row, y, c = lax.axis_index("row"), lax.axis_index("col"), lax.axis_index("depth")
    z, x = row // NX, lax.rem(row, NX)
    g, wp, wr, ws = (g0, g1, g2), (wp0, wp1, wp2), (wr0, wr1, wr2), (ws0, ws1, ws2)
    last = len(CHUNKS) - 1

    def at(x_=x, y_=y, z_=z, c_=c):
        return (z_ * NX + x_, y_, c_)

    def turn(value, by, n):
        return lax.rem(value + (by + n), n)

    sends, locals_ = [], []

    def send(src, dst, device):
        i = len(sends)
        copy = pltpu.make_async_remote_copy(
            src_ref=src, dst_ref=dst, send_sem=send_sem.at[i], recv_sem=recv_sem.at[i],
            device_id=device, device_id_type=pl.DeviceIdType.MESH,
        )
        copy.start()
        sends.append(copy)
        return copy

    def local(src, dst):
        copy = pltpu.make_async_copy(src, dst, local_sem.at[len(locals_)])
        copy.start()
        locals_.append(copy)
        return copy

    partners = [at(x_=turn(x, o, NX)) for o in (1, 2, 3)]
    partners += [at(y_=turn(y, o, NY)) for o in (1, 2, 3)]
    partners += [at(z_=turn(z, o, NZ)) for o in (1, -1)]
    partners += [at(c_=1 - c)]
    barrier = pltpu.get_barrier_semaphore()
    for device in partners:
        pl.semaphore_signal(barrier, inc=1, device_id=device, device_id_type=pl.DeviceIdType.MESH)

    loads = [
        local(src, dst)
        for src, dst in ((gate_hbm, gate_ref), (up_hbm, up_ref), (grad_hbm, grad_ref), (x_hbm, x_ref))
    ]
    w_loads = [
        local(
            (gw_hbm, uw_hbm)[which].at[pl.ds(first, columns)],
            own_w.at[block, pl.ds(there, columns)],
        )
        for which, first, block, there, columns in PIECES
    ]
    for block, first, end in ROW_PADS:
        own_w[block, first:end, :] = jnp.zeros((end - first, WIDE), BF)
    for block, first, end in PADS:
        own_g[block, :, first:end] = jnp.zeros((ROWS, end - first), BF)
    for load in loads[:3]:
        load.wait()

    done = set()

    def gated(k):
        for t in range(TILES):
            chunks = [(tile % (XB // WIDE)) * WIDE // CHUNKS[0] for tile in (t, TILES + t)]
            if k not in chunks or t in done:
                continue
            done.add(t)
            n = min(WIDE, UNITS - t * WIDE)
            cut = slice(t * WIDE, t * WIDE + n)
            gate = gate_ref[:, cut].astype(F32)
            grad = grad_ref[:, cut].astype(F32)
            sigma = 1.0 / (1.0 + jnp.exp(-gate))
            scaled = grad * sigma
            values = (
                scaled * up_ref[:, cut].astype(F32) * (1.0 + gate * (1.0 - sigma)), scaled * gate
            )
            for tile, value in zip((t, TILES + t), values):
                block, first = divmod(tile * WIDE, XB)
                own_g[block, :, first:first + n] = value.astype(BF)

    gated(0)
    pl.semaphore_wait(barrier, len(partners))

    def slab(of):
        return pl.ds(pl.multiple_of((z * NX + of) * ROWS, 16), ROWS)

    mates = {1: x + 1 - 2 * lax.rem(x, 2), 2: turn(x, 2, NX), 3: 3 - x}
    swapped, first_hop = [], {}

    def swap(k):
        cols = pl.ds(STARTS[k], CHUNKS[k])
        for way in (1, -1):
            first_hop[k, way] = send(
                own_g.at[x, :, cols], g[k].at[slab(x)], at(z_=turn(z, way, NZ))
            )
        copies = {}
        for m in (1, 3, 2):
            copies[m] = send(own_g.at[mates[m], :, cols], g[k].at[slab(x)], at(x_=mates[m]))
        swapped.append((copies, local(own_g.at[x, :, cols], g[k].at[slab(x)])))

    def arrived(k):
        copies, copy = swapped[k]
        for m in (1, 2, 3):
            copies[m].wait_recv()
        copy.wait()

    near, far = [(h, s) for h in (1, 2, 3) for s in (0, 1)], [(h, s) for h in (1, 2, 3) for s in (1, 0)]
    items = {1: [], -1: [(0, h, s) for h, s in near]}
    for k in range(len(CHUNKS)):
        items[1] += [(k, h, s) for h, s in near + [(4, 0)]]
        if k:
            items[-1] += [(k, h, s) for h, s in far + [(4, 1)]]
    items[-1].insert(7, (0, 4, 1))
    events = 7
    moved = {1: [], -1: []}

    def pass_on(i, way):
        if i >= len(items[way]):
            return
        k, hop, half = items[way][i]
        to = at(z_=turn(z, way, NZ))
        if (hop, half) == (1, 0):
            rows = slab(mates[1])
            moved[way].append((first_hop[k, way], send(g[k].at[rows], g[k].at[rows], to)))
            return
        block = turn(z, -way * (hop - 1), NZ)
        part_ = x // 2 if half == 0 else 1 - x // 2
        rows = pl.ds(pl.multiple_of(block * ZB + part_ * (ZB // 2), 16), ZB // 2)
        moved[way].append((send(g[k].at[rows], g[k].at[rows], to),))

    swap(0)
    loads[3].wait()
    xt_own[...] = x_ref[...].astype(F32).T.astype(BF)
    xt_rows = pl.ds(pl.multiple_of(x * WIDE, WIDE), WIDE)
    xt_cols = pl.ds(pl.multiple_of(y * TB, 128), TB)
    xt_x = [send(xt_own, xt.at[xt_rows, xt_cols], at(x_=turn(x, o, NX))) for o in (1, 2, 3)]
    xt_local = local(xt_own, xt.at[xt_rows, xt_cols])
    gated(1)
    swap(1)
    swapped[0][0][1].wait_recv()
    for way in (1, -1):
        pass_on(0, way)
    gated(2)
    for m in (2, 3):
        swapped[0][0][m].wait_recv()
    swapped[0][1].wait()
    for way in (1, -1):
        pass_on(1, way)
    for copy in xt_x:
        copy.wait_recv()
    xt_local.wait()
    xt_y = [send(xt.at[:, xt_cols], xt.at[:, xt_cols], at(y_=turn(y, o, NY))) for o in (1, 2, 3)]
    for load in w_loads:
        load.wait()

    w_half = pl.ds(pl.multiple_of(c * (XB // 2), 64), XB // 2)
    w_cols = pl.ds(pl.multiple_of(x * WIDE, WIDE), WIDE)
    w_sent = [
        send(
            own_w.at[turn(x, o, NX), w_half], w_all.at[w_half, w_cols], at(x_=turn(x, o, NX))
        )
        for o in (1, 2, 3)
    ]
    w_local = local(own_w.at[x, w_half], w_all.at[w_half, w_cols])
    swap(2)

    def weight_piece(k, lo):
        n = min(256, CHUNKS[k] - lo)
        value = jnp.dot(xt[...], g[k][:, lo:lo + n], preferred_element_type=F32).astype(BF)
        for b in range(NX):
            for h in range(NC):
                wp[k][h, b * HALF:(b + 1) * HALF, lo:lo + n] = value[
                    b * WIDE + h * HALF:b * WIDE + (h + 1) * HALF
                ]

    exchanged = {}

    def exchange(k):
        exchanged[k] = send(wp[k].at[1 - c], wr[k], at(c_=1 - c))

    returned = []

    def give_back(k):
        exchanged[k].wait_recv()
        ws[k][...] = (wp[k][c].astype(F32) + wr[k][...].astype(F32)).astype(BF)
        cols = pl.ds(STARTS[k], CHUNKS[k])

        def rows(of):
            return pl.ds(pl.multiple_of(of * HALF, HALF), HALF)

        for o in (1, 2, 3):
            to = turn(x, o, NX)
            returned.append(send(ws[k].at[rows(to)], w_out.at[x, :, cols], at(x_=to)).wait_recv)
        returned.append(local(ws[k].at[rows(x)], w_out.at[x, :, cols]).wait)

    partial, scattered = {}, []

    def rows_of(b):
        return pl.ds(pl.multiple_of(turn(z, b, NZ) * ZB, 64), ZB)

    def input_part(b):
        rows = rows_of(b)
        total = None
        for k in range(len(CHUNKS)):
            term = jnp.dot(
                g[k][rows, :], w_all[STARTS[k]:STARTS[k] + CHUNKS[k], :],
                preferred_element_type=F32,
            )
            total = term if total is None else total + term
        for b_ in range(NX):
            part[b_, rows, :] = total[:, b_ * WIDE:(b_ + 1) * WIDE].astype(BF)
        partial[b] = [
            send(part.at[turn(x, o, NX), rows], part_in.at[o - 1, rows], at(x_=turn(x, o, NX)))
            for o in (1, 2, 3)
        ]

    def input_sum(b):
        rows = rows_of(b)
        for copy in partial[b]:
            copy.wait_recv()
        total = part[x, rows, :].astype(F32)
        for o in range(3):
            total = total + part_in[o, rows, :].astype(F32)
        summed[rows, :] = total.astype(BF)
        block = turn(z, b, NZ)
        owner, parity = block // 2, lax.rem(block, 2)
        away = turn(owner - y, 0, NY)
        copy = pltpu.make_async_remote_copy(
            src_ref=summed.at[rows],
            dst_ref=summed_in.at[lax.rem(away + 3, NY), pl.ds(pl.multiple_of(parity * ZB, 64), ZB)],
            send_sem=y_send.at[b + 3], recv_sem=y_recv.at[2 * away + parity],
            device_id=at(y_=owner), device_id_type=pl.DeviceIdType.MESH,
        )
        scattered.append((away, copy))

        @pl.when(away != 0)
        def _():
            copy.start()

    over_core = []
    parts_at = {(1, 6): (0,), (2, 1): (-1, 1), (2, 3): (-2, 2), (2, 5): (-3, 3), (2, 6): (4,)}
    sums_at = {(2, 1): (0,), (2, 4): (-1, 1)}
    for k in range(len(CHUNKS)):
        for e in range(events):
            if e == 4 and k < last:
                arrived(k + 1)
            for way in (1, -1):
                for copy in moved[way][k * events + e]:
                    copy.wait_recv()
                pass_on(k * events + e + 2, way)
            if (k, e) == (1, 2):
                for copy in xt_y:
                    copy.wait_recv()
            if (k, e) == (1, 4):
                for copy in w_sent:
                    copy.wait_recv()
                w_local.wait()
                over_core.append(send(w_all.at[w_half], w_all.at[w_half], at(c_=1 - c)))
            if (k, e) == (1, 6):
                over_core[0].wait_recv()
            for b in parts_at.get((k, e), ()):
                input_part(b)
            if k >= 1:
                piece = e - (2 if k == 1 else 0)
                if 0 <= piece < 3 and piece * 256 < CHUNKS[k - 1]:
                    weight_piece(k - 1, piece * 256)
                if piece == 2:
                    exchange(k - 1)
                if piece == (4 if k == 1 else 3):
                    give_back(k - 1)
            for b in sums_at.get((k, e), ()):
                input_sum(b)

    for lo in range(0, CHUNKS[last], 256):
        weight_piece(last, lo)
    exchange(last)
    for b in (-2, 2):
        input_sum(b)
    give_back(last)
    for b in (-3, 3, 4):
        input_sum(b)

    for o in (1, 2, 3):
        for parity in (0, 1):
            landed = summed_in.at[o - 1, pl.ds(parity * ZB, ZB)]
            pltpu.make_async_remote_copy(
                src_ref=landed, dst_ref=landed,
                send_sem=y_send.at[0], recv_sem=y_recv.at[2 * o + parity],
                device_id=at(y_=turn(y, o, NY)), device_id_type=pl.DeviceIdType.MESH,
            ).wait_recv()
    total = summed[pl.ds(pl.multiple_of(y * TB, 128), TB), :].astype(F32)
    for o in range(3):
        total = total + summed_in[o].astype(F32)
    ig_ref[...] = total.astype(BF)

    for wait in returned:
        wait()
    for copy in sends:
        copy.wait_send()
    for away, copy in scattered:
        pl.when(away != 0)(copy.wait_send)


def unpack(ig_in, w_out, ig_ref, go_ref, uo_ref):
    ig_ref[...] = ig_in[...]
    for which, first, block, there, columns in PIECES:
        target = (go_ref, uo_ref)[which]
        target[:, first:first + columns] = w_out[block, :, there:there + columns]


def on_device(layer_input, gate_pre, up_pre, hidden_grad, gate_weight, up_weight):
    vmem = pltpu.VMEM
    scratch = [vmem((TB, WIDE), BF)] + [vmem((ROWS, UNITS), BF)] * 3 + [vmem((NX, ROWS, XB), BF)]
    scratch += [vmem((LAYER, w), BF) for w in CHUNKS]
    scratch += [
        vmem((NX, XB, WIDE), BF),
        vmem((XB, DB), BF),
        vmem((WIDE, TB), BF),
        vmem((DB, LAYER), BF),
        vmem((NX, LAYER, WIDE), BF),
        vmem((NX - 1, LAYER, WIDE), BF),
        vmem((LAYER, WIDE), BF),
        vmem((NY, TB, WIDE), BF),
    ]
    scratch += [vmem((NC, NX * HALF, w), BF) for w in CHUNKS]
    scratch += [vmem((NX * HALF, w), BF) for w in CHUNKS]
    scratch += [vmem((NX * HALF, w), BF) for w in CHUNKS]
    scratch += [
        pltpu.SemaphoreType.DMA((N_COPIES,)),
        pltpu.SemaphoreType.DMA((N_COPIES,)),
        pltpu.SemaphoreType.DMA((20,)),
        pltpu.SemaphoreType.DMA((NZ,)),
        pltpu.SemaphoreType.DMA((2 * NY,)),
    ]
    in_vmem = pl.BlockSpec(memory_space=pltpu.VMEM)
    anywhere = pl.BlockSpec(memory_space=pl.ANY)
    input_grad, packed = pl.pallas_call(
        kernel,
        out_shape=(
            jax.ShapeDtypeStruct((TB, WIDE), BF),
            jax.ShapeDtypeStruct((NX, HALF, XB), BF),
        ),
        in_specs=[anywhere] * 6,
        out_specs=(in_vmem, anywhere),
        scratch_shapes=scratch,
        compiler_params=pltpu.CompilerParams(
            collective_id=0, has_side_effects=True, vmem_limit_bytes=56 * 1024 * 1024
        ),
    )(layer_input, gate_pre, up_pre, hidden_grad, gate_weight.T, up_weight.T)
    return pl.pallas_call(
        unpack,
        out_shape=(
            jax.ShapeDtypeStruct((TB, WIDE), BF),
            jax.ShapeDtypeStruct((HALF, UNITS), BF),
            jax.ShapeDtypeStruct((HALF, UNITS), BF),
        ),
        in_specs=[in_vmem] * 2,
        out_specs=(in_vmem,) * 3,
    )(input_grad, packed)


def solution(mesh):
    placed = (
        P(("depth", "col"), "row"),
        P(("depth", "row"), "col"),
        P(("depth", "row"), "col"),
        P(("depth", "row"), "col"),
        P("row", "col"),
        P("row", "col"),
    )
    return jax.shard_map(
        on_device,
        mesh=mesh,
        in_specs=placed,
        out_specs=(
            P(("depth", "col"), "row"),
            P(("row", "depth"), "col"),
            P(("row", "depth"), "col"),
        ),
        check_vma=False,
    )
```

```python
import jax
import jax.numpy as jnp
from jax import lax
from jax.experimental import pallas as pl
from jax.experimental.pallas import tpu as pltpu
from jax.sharding import PartitionSpec as P

NX, NY, NZ, NC = 4, 4, 8, 2
ROWS = 48
ZB = NX * ROWS
LAYER = NZ * ZB
UNITS = 3696
XB = 1920
TILES = 29
WIDE = 128
DB = NX * WIDE
TB = 2 * ZB
HALF = WIDE // 2
CHUNKS = (640, 640, 640)
STARTS = (0, 640, 1280)
N_COPIES = 112
BF, F32 = jnp.bfloat16, jnp.float32

PIECES = (
    (0, 0, 0, 0, 1920),
    (0, 1920, 1, 0, 1776),
    (1, 0, 1, 1792, 128),
    (1, 128, 2, 0, 1920),
    (1, 2048, 3, 0, 1648),
)
PADS = ((1, 1664, 1792), (3, 1536, 1920))
ROW_PADS = ((1, 1776, 1792), (3, 1648, 1920))


def kernel(
    x_hbm, gate_hbm, up_hbm, grad_hbm, gw_hbm, uw_hbm,
    ig_ref, w_out,
    x_ref, gate_ref, up_ref, grad_ref, own_g, g0, g1, g2, own_w, w_all, xt_own, xt, part, part_in, summed, summed_in,
    wp0, wp1, wp2, wr0, wr1, wr2, ws0, ws1, ws2,
    send_sem, recv_sem, local_sem, y_send, y_recv,
):
    row, y, c = lax.axis_index("row"), lax.axis_index("col"), lax.axis_index("depth")
    z, x = row // NX, lax.rem(row, NX)
    g, wp, wr, ws = (g0, g1, g2), (wp0, wp1, wp2), (wr0, wr1, wr2), (ws0, ws1, ws2)
    last = len(CHUNKS) - 1

    def at(x_=x, y_=y, z_=z, c_=c):
        return (z_ * NX + x_, y_, c_)

    def turn(value, by, n):
        return lax.rem(value + (by + n), n)

    sends, locals_ = [], []

    def send(src, dst, device):
        i = len(sends)
        copy = pltpu.make_async_remote_copy(
            src_ref=src, dst_ref=dst, send_sem=send_sem.at[i], recv_sem=recv_sem.at[i],
            device_id=device, device_id_type=pl.DeviceIdType.MESH,
        )
        copy.start()
        sends.append(copy)
        return copy

    def local(src, dst):
        copy = pltpu.make_async_copy(src, dst, local_sem.at[len(locals_)])
        copy.start()
        locals_.append(copy)
        return copy

    loads = [
        local(src, dst)
        for src, dst in ((gate_hbm, gate_ref), (up_hbm, up_ref), (grad_hbm, grad_ref), (x_hbm, x_ref))
    ]
    partners = [at(x_=turn(x, o, NX)) for o in (1, 2, 3)]
    partners += [at(y_=turn(y, o, NY)) for o in (1, 2, 3)]
    partners += [at(z_=turn(z, o, NZ)) for o in (1, -1)]
    partners += [at(c_=1 - c)]
    barrier = pltpu.get_barrier_semaphore()
    for device in partners:
        pl.semaphore_signal(barrier, inc=1, device_id=device, device_id_type=pl.DeviceIdType.MESH)

    for block, first, end in PADS:
        own_g[block, :, first:end] = jnp.zeros((ROWS, end - first), BF)
    for load in loads[:3]:
        load.wait()

    done = set()

    def gated(k):
        for t in range(TILES):
            chunks = [(tile % (XB // WIDE)) * WIDE // CHUNKS[0] for tile in (t, TILES + t)]
            if k not in chunks or t in done:
                continue
            done.add(t)
            n = min(WIDE, UNITS - t * WIDE)
            cut = slice(t * WIDE, t * WIDE + n)
            gate = gate_ref[:, cut].astype(F32)
            grad = grad_ref[:, cut].astype(F32)
            sigma = 1.0 / (1.0 + jnp.exp(-gate))
            scaled = grad * sigma
            values = (
                scaled * up_ref[:, cut].astype(F32) * (1.0 + gate * (1.0 - sigma)), scaled * gate
            )
            for tile, value in zip((t, TILES + t), values):
                block, first = divmod(tile * WIDE, XB)
                own_g[block, :, first:first + n] = value.astype(BF)

    gated(0)
    pl.semaphore_wait(barrier, len(partners))

    def slab(of):
        return pl.ds(pl.multiple_of((z * NX + of) * ROWS, 16), ROWS)

    mates = {1: x + 1 - 2 * lax.rem(x, 2), 2: turn(x, 2, NX), 3: 3 - x}
    swapped, first_hop = [], {}

    def swap(k):
        cols = pl.ds(STARTS[k], CHUNKS[k])
        for way in (1, -1):
            first_hop[k, way] = send(
                own_g.at[x, :, cols], g[k].at[slab(x)], at(z_=turn(z, way, NZ))
            )
        copies = {}
        for m in (1, 3, 2):
            copies[m] = send(own_g.at[mates[m], :, cols], g[k].at[slab(x)], at(x_=mates[m]))
        swapped.append((copies, local(own_g.at[x, :, cols], g[k].at[slab(x)])))

    def arrived(k):
        copies, copy = swapped[k]
        for m in (1, 2, 3):
            copies[m].wait_recv()
        copy.wait()

    near, far = [(h, s) for h in (1, 2, 3) for s in (0, 1)], [(h, s) for h in (1, 2, 3) for s in (1, 0)]
    items = {1: [], -1: [(0, h, s) for h, s in near]}
    for k in range(len(CHUNKS)):
        items[1] += [(k, h, s) for h, s in near + [(4, 0)]]
        if k:
            items[-1] += [(k, h, s) for h, s in far + [(4, 1)]]
    items[-1].insert(7, (0, 4, 1))
    events = 7
    moved = {1: [], -1: []}

    def pass_on(i, way):
        if i >= len(items[way]):
            return
        k, hop, half = items[way][i]
        to = at(z_=turn(z, way, NZ))
        if (hop, half) == (1, 0):
            rows = slab(mates[1])
            moved[way].append((first_hop[k, way], send(g[k].at[rows], g[k].at[rows], to)))
            return
        block = turn(z, -way * (hop - 1), NZ)
        part_ = x // 2 if half == 0 else 1 - x // 2
        rows = pl.ds(pl.multiple_of(block * ZB + part_ * (ZB // 2), 16), ZB // 2)
        moved[way].append((send(g[k].at[rows], g[k].at[rows], to),))

    swap(0)
    w_loads = [
        local(
            (gw_hbm, uw_hbm)[which].at[pl.ds(first, columns)],
            own_w.at[block, pl.ds(there, columns)],
        )
        for which, first, block, there, columns in PIECES
    ]
    for block, first, end in ROW_PADS:
        own_w[block, first:end, :] = jnp.zeros((end - first, WIDE), BF)
    loads[3].wait()
    xt_own[...] = x_ref[...].astype(F32).T.astype(BF)
    xt_rows = pl.ds(pl.multiple_of(x * WIDE, WIDE), WIDE)
    xt_cols = pl.ds(pl.multiple_of(y * TB, 128), TB)
    xt_x = [send(xt_own, xt.at[xt_rows, xt_cols], at(x_=turn(x, o, NX))) for o in (1, 2, 3)]
    xt_local = local(xt_own, xt.at[xt_rows, xt_cols])
    gated(1)
    swap(1)
    swapped[0][0][1].wait_recv()
    for way in (1, -1):
        pass_on(0, way)
    gated(2)
    for m in (2, 3):
        swapped[0][0][m].wait_recv()
    swapped[0][1].wait()
    for way in (1, -1):
        pass_on(1, way)
    for copy in xt_x:
        copy.wait_recv()
    xt_local.wait()
    xt_y = [send(xt.at[:, xt_cols], xt.at[:, xt_cols], at(y_=turn(y, o, NY))) for o in (1, 2, 3)]
    for load in w_loads:
        load.wait()

    w_half = pl.ds(pl.multiple_of(c * (XB // 2), 64), XB // 2)
    w_cols = pl.ds(pl.multiple_of(x * WIDE, WIDE), WIDE)
    w_sent = [
        send(
            own_w.at[turn(x, o, NX), w_half], w_all.at[w_half, w_cols], at(x_=turn(x, o, NX))
        )
        for o in (1, 2, 3)
    ]
    w_local = local(own_w.at[x, w_half], w_all.at[w_half, w_cols])
    swap(2)

    def weight_piece(k, lo):
        n = min(256, CHUNKS[k] - lo)
        value = jnp.dot(xt[...], g[k][:, lo:lo + n], preferred_element_type=F32).astype(BF)
        for b in range(NX):
            for h in range(NC):
                wp[k][h, b * HALF:(b + 1) * HALF, lo:lo + n] = value[
                    b * WIDE + h * HALF:b * WIDE + (h + 1) * HALF
                ]

    exchanged = {}

    def exchange(k):
        exchanged[k] = send(wp[k].at[1 - c], wr[k], at(c_=1 - c))

    returned = []

    def give_back(k):
        exchanged[k].wait_recv()
        ws[k][...] = (wp[k][c].astype(F32) + wr[k][...].astype(F32)).astype(BF)
        cols = pl.ds(STARTS[k], CHUNKS[k])

        def rows(of):
            return pl.ds(pl.multiple_of(of * HALF, HALF), HALF)

        for o in (1, 2, 3):
            to = turn(x, o, NX)
            returned.append(send(ws[k].at[rows(to)], w_out.at[x, :, cols], at(x_=to)).wait_recv)
        returned.append(local(ws[k].at[rows(x)], w_out.at[x, :, cols]).wait)

    partial, scattered = {}, []

    def rows_of(b):
        return pl.ds(pl.multiple_of(turn(z, b, NZ) * ZB, 64), ZB)

    def input_part(b):
        rows = rows_of(b)
        total = None
        for k in range(len(CHUNKS)):
            term = jnp.dot(
                g[k][rows, :], w_all[STARTS[k]:STARTS[k] + CHUNKS[k], :],
                preferred_element_type=F32,
            )
            total = term if total is None else total + term
        for b_ in range(NX):
            part[b_, rows, :] = total[:, b_ * WIDE:(b_ + 1) * WIDE].astype(BF)
        partial[b] = [
            send(part.at[turn(x, o, NX), rows], part_in.at[o - 1, rows], at(x_=turn(x, o, NX)))
            for o in (1, 2, 3)
        ]

    def input_sum(b):
        rows = rows_of(b)
        for copy in partial[b]:
            copy.wait_recv()
        total = part[x, rows, :].astype(F32)
        for o in range(3):
            total = total + part_in[o, rows, :].astype(F32)
        summed[rows, :] = total.astype(BF)
        block = turn(z, b, NZ)
        owner, parity = block // 2, lax.rem(block, 2)
        away = turn(owner - y, 0, NY)
        copy = pltpu.make_async_remote_copy(
            src_ref=summed.at[rows],
            dst_ref=summed_in.at[lax.rem(away + 3, NY), pl.ds(pl.multiple_of(parity * ZB, 64), ZB)],
            send_sem=y_send.at[b + 3], recv_sem=y_recv.at[2 * away + parity],
            device_id=at(y_=owner), device_id_type=pl.DeviceIdType.MESH,
        )
        scattered.append((away, copy))

        @pl.when(away != 0)
        def _():
            copy.start()

    over_core = []
    parts_at = {(1, 6): (0,), (2, 1): (-1, 1), (2, 3): (-2, 2), (2, 5): (-3, 3), (2, 6): (4,)}
    sums_at = {(2, 1): (0,), (2, 4): (-1, 1)}
    for k in range(len(CHUNKS)):
        for e in range(events):
            if e == 4 and k < last:
                arrived(k + 1)
            for way in (1, -1):
                for copy in moved[way][k * events + e]:
                    copy.wait_recv()
                pass_on(k * events + e + 2, way)
            if (k, e) == (1, 2):
                for copy in xt_y:
                    copy.wait_recv()
            if (k, e) == (1, 4):
                for copy in w_sent:
                    copy.wait_recv()
                w_local.wait()
                over_core.append(send(w_all.at[w_half], w_all.at[w_half], at(c_=1 - c)))
            if (k, e) == (1, 6):
                over_core[0].wait_recv()
            for b in parts_at.get((k, e), ()):
                input_part(b)
            if k >= 1:
                piece = e - (2 if k == 1 else 0)
                if 0 <= piece < 3 and piece * 256 < CHUNKS[k - 1]:
                    weight_piece(k - 1, piece * 256)
                if piece == 2:
                    exchange(k - 1)
                if piece == (4 if k == 1 else 3):
                    give_back(k - 1)
            for b in sums_at.get((k, e), ()):
                input_sum(b)

    for lo in range(0, CHUNKS[last], 256):
        weight_piece(last, lo)
    exchange(last)
    for b in (-2, 2):
        input_sum(b)
    give_back(last)
    for b in (-3, 3, 4):
        input_sum(b)

    for o in (1, 2, 3):
        for parity in (0, 1):
            landed = summed_in.at[o - 1, pl.ds(parity * ZB, ZB)]
            pltpu.make_async_remote_copy(
                src_ref=landed, dst_ref=landed,
                send_sem=y_send.at[0], recv_sem=y_recv.at[2 * o + parity],
                device_id=at(y_=turn(y, o, NY)), device_id_type=pl.DeviceIdType.MESH,
            ).wait_recv()
    total = summed[pl.ds(pl.multiple_of(y * TB, 128), TB), :].astype(F32)
    for o in range(3):
        total = total + summed_in[o].astype(F32)
    ig_ref[...] = total.astype(BF)

    for wait in returned:
        wait()
    for copy in sends:
        copy.wait_send()
    for away, copy in scattered:
        pl.when(away != 0)(copy.wait_send)


def unpack(ig_in, w_out, ig_ref, go_ref, uo_ref):
    ig_ref[...] = ig_in[...]
    for which, first, block, there, columns in PIECES:
        target = (go_ref, uo_ref)[which]
        target[:, first:first + columns] = w_out[block, :, there:there + columns]


def on_device(layer_input, gate_pre, up_pre, hidden_grad, gate_weight, up_weight):
    vmem = pltpu.VMEM
    scratch = [vmem((TB, WIDE), BF)] + [vmem((ROWS, UNITS), BF)] * 3 + [vmem((NX, ROWS, XB), BF)]
    scratch += [vmem((LAYER, w), BF) for w in CHUNKS]
    scratch += [
        vmem((NX, XB, WIDE), BF),
        vmem((XB, DB), BF),
        vmem((WIDE, TB), BF),
        vmem((DB, LAYER), BF),
        vmem((NX, LAYER, WIDE), BF),
        vmem((NX - 1, LAYER, WIDE), BF),
        vmem((LAYER, WIDE), BF),
        vmem((NY, TB, WIDE), BF),
    ]
    scratch += [vmem((NC, NX * HALF, w), BF) for w in CHUNKS]
    scratch += [vmem((NX * HALF, w), BF) for w in CHUNKS]
    scratch += [vmem((NX * HALF, w), BF) for w in CHUNKS]
    scratch += [
        pltpu.SemaphoreType.DMA((N_COPIES,)),
        pltpu.SemaphoreType.DMA((N_COPIES,)),
        pltpu.SemaphoreType.DMA((20,)),
        pltpu.SemaphoreType.DMA((NZ,)),
        pltpu.SemaphoreType.DMA((2 * NY,)),
    ]
    in_vmem = pl.BlockSpec(memory_space=pltpu.VMEM)
    anywhere = pl.BlockSpec(memory_space=pl.ANY)
    input_grad, packed = pl.pallas_call(
        kernel,
        out_shape=(
            jax.ShapeDtypeStruct((TB, WIDE), BF),
            jax.ShapeDtypeStruct((NX, HALF, XB), BF),
        ),
        in_specs=[anywhere] * 6,
        out_specs=(in_vmem, anywhere),
        scratch_shapes=scratch,
        compiler_params=pltpu.CompilerParams(
            collective_id=0, has_side_effects=True, vmem_limit_bytes=56 * 1024 * 1024
        ),
    )(layer_input, gate_pre, up_pre, hidden_grad, gate_weight.T, up_weight.T)
    return pl.pallas_call(
        unpack,
        out_shape=(
            jax.ShapeDtypeStruct((TB, WIDE), BF),
            jax.ShapeDtypeStruct((HALF, UNITS), BF),
            jax.ShapeDtypeStruct((HALF, UNITS), BF),
        ),
        grid=(2,),
        in_specs=[
            pl.BlockSpec((TB // 2, WIDE), lambda i: (i, 0)),
            pl.BlockSpec((NX, HALF // 2, XB), lambda i: (0, i, 0)),
        ],
        out_specs=(
            pl.BlockSpec((TB // 2, WIDE), lambda i: (i, 0)),
            pl.BlockSpec((HALF // 2, UNITS), lambda i: (i, 0)),
            pl.BlockSpec((HALF // 2, UNITS), lambda i: (i, 0)),
        ),
    )(input_grad, packed)


def solution(mesh):
    placed = (
        P(("depth", "col"), "row"),
        P(("depth", "row"), "col"),
        P(("depth", "row"), "col"),
        P(("depth", "row"), "col"),
        P("row", "col"),
        P("row", "col"),
    )
    return jax.shard_map(
        on_device,
        mesh=mesh,
        in_specs=placed,
        out_specs=(
            P(("depth", "col"), "row"),
            P(("row", "depth"), "col"),
            P(("row", "depth"), "col"),
        ),
        check_vma=False,
    )
```

```python
import jax
import jax.numpy as jnp
from jax import lax
from jax.experimental import pallas as pl
from jax.experimental.pallas import tpu as pltpu
from jax.sharding import PartitionSpec as P

NX, NY, NZ, NC = 4, 4, 8, 2
ROWS = 48
ZB = NX * ROWS
LAYER = NZ * ZB
UNITS = 3696
XB = 1920
TILES = 29
WIDE = 128
DB = NX * WIDE
TB = 2 * ZB
HALF = WIDE // 2
CHUNKS = (640, 512, 768)
STARTS = (0, 640, 1152)
N_COPIES = 112
BF, F32 = jnp.bfloat16, jnp.float32

PIECES = (
    (0, 0, 0, 0, 1920),
    (0, 1920, 1, 0, 1776),
    (1, 0, 1, 1792, 128),
    (1, 128, 2, 0, 1920),
    (1, 2048, 3, 0, 1648),
)
PADS = ((1, 1664, 1792), (3, 1536, 1920))
ROW_PADS = ((1, 1776, 1792), (3, 1648, 1920))


def kernel(
    x_hbm, gate_hbm, up_hbm, grad_hbm, gw_hbm, uw_hbm,
    ig_ref, w_out,
    x_ref, gate_ref, up_ref, grad_ref, own_g, g0, g1, g2, own_w, w_all, xt_own, xt, part, part_in, summed, summed_in,
    wp0, wp1, wp2, wr0, wr1, wr2, ws0, ws1, ws2,
    send_sem, recv_sem, local_sem, y_send, y_recv,
):
    row, y, c = lax.axis_index("row"), lax.axis_index("col"), lax.axis_index("depth")
    z, x = row // NX, lax.rem(row, NX)
    g, wp, wr, ws = (g0, g1, g2), (wp0, wp1, wp2), (wr0, wr1, wr2), (ws0, ws1, ws2)
    last = len(CHUNKS) - 1

    def at(x_=x, y_=y, z_=z, c_=c):
        return (z_ * NX + x_, y_, c_)

    def turn(value, by, n):
        return lax.rem(value + (by + n), n)

    sends, locals_ = [], []

    def send(src, dst, device):
        i = len(sends)
        copy = pltpu.make_async_remote_copy(
            src_ref=src, dst_ref=dst, send_sem=send_sem.at[i], recv_sem=recv_sem.at[i],
            device_id=device, device_id_type=pl.DeviceIdType.MESH,
        )
        copy.start()
        sends.append(copy)
        return copy

    def local(src, dst):
        copy = pltpu.make_async_copy(src, dst, local_sem.at[len(locals_)])
        copy.start()
        locals_.append(copy)
        return copy

    loads = [
        local(src, dst)
        for src, dst in ((gate_hbm, gate_ref), (up_hbm, up_ref), (grad_hbm, grad_ref), (x_hbm, x_ref))
    ]
    partners = [at(x_=turn(x, o, NX)) for o in (1, 2, 3)]
    partners += [at(y_=turn(y, o, NY)) for o in (1, 2, 3)]
    partners += [at(z_=turn(z, o, NZ)) for o in (1, -1)]
    partners += [at(c_=1 - c)]
    barrier = pltpu.get_barrier_semaphore()
    for device in partners:
        pl.semaphore_signal(barrier, inc=1, device_id=device, device_id_type=pl.DeviceIdType.MESH)

    for block, first, end in PADS:
        own_g[block, :, first:end] = jnp.zeros((ROWS, end - first), BF)
    for load in loads[:3]:
        load.wait()

    done = set()

    def gated(k):
        for t in range(TILES):
            places = [tile % (XB // WIDE) * WIDE for tile in (t, TILES + t)]
            chunks = [sum(start <= place for start in STARTS) - 1 for place in places]
            if k not in chunks or t in done:
                continue
            done.add(t)
            n = min(WIDE, UNITS - t * WIDE)
            cut = slice(t * WIDE, t * WIDE + n)
            gate = gate_ref[:, cut].astype(F32)
            grad = grad_ref[:, cut].astype(F32)
            sigma = 1.0 / (1.0 + jnp.exp(-gate))
            scaled = grad * sigma
            values = (
                scaled * up_ref[:, cut].astype(F32) * (1.0 + gate * (1.0 - sigma)), scaled * gate
            )
            for tile, value in zip((t, TILES + t), values):
                block, first = divmod(tile * WIDE, XB)
                own_g[block, :, first:first + n] = value.astype(BF)

    gated(0)
    pl.semaphore_wait(barrier, len(partners))

    def slab(of):
        return pl.ds(pl.multiple_of((z * NX + of) * ROWS, 16), ROWS)

    mates = {1: x + 1 - 2 * lax.rem(x, 2), 2: turn(x, 2, NX), 3: 3 - x}
    swapped, first_hop = [], {}

    def swap(k):
        cols = pl.ds(STARTS[k], CHUNKS[k])
        for way in (1, -1):
            first_hop[k, way] = send(
                own_g.at[x, :, cols], g[k].at[slab(x)], at(z_=turn(z, way, NZ))
            )
        copies = {}
        for m in (1, 3, 2):
            copies[m] = send(own_g.at[mates[m], :, cols], g[k].at[slab(x)], at(x_=mates[m]))
        swapped.append((copies, local(own_g.at[x, :, cols], g[k].at[slab(x)])))

    def arrived(k):
        copies, copy = swapped[k]
        for m in (1, 2, 3):
            copies[m].wait_recv()
        copy.wait()

    near, far = [(h, s) for h in (1, 2, 3) for s in (0, 1)], [(h, s) for h in (1, 2, 3) for s in (1, 0)]
    items = {1: [], -1: [(0, h, s) for h, s in near]}
    for k in range(len(CHUNKS)):
        items[1] += [(k, h, s) for h, s in near + [(4, 0)]]
        if k:
            items[-1] += [(k, h, s) for h, s in far + [(4, 1)]]
    items[-1].insert(7, (0, 4, 1))
    events = 7
    moved = {1: [], -1: []}

    def pass_on(i, way):
        if i >= len(items[way]):
            return
        k, hop, half = items[way][i]
        to = at(z_=turn(z, way, NZ))
        if (hop, half) == (1, 0):
            rows = slab(mates[1])
            moved[way].append((first_hop[k, way], send(g[k].at[rows], g[k].at[rows], to)))
            return
        block = turn(z, -way * (hop - 1), NZ)
        part_ = x // 2 if half == 0 else 1 - x // 2
        rows = pl.ds(pl.multiple_of(block * ZB + part_ * (ZB // 2), 16), ZB // 2)
        moved[way].append((send(g[k].at[rows], g[k].at[rows], to),))

    swap(0)
    w_loads = [
        local(
            (gw_hbm, uw_hbm)[which].at[pl.ds(first, columns)],
            own_w.at[block, pl.ds(there, columns)],
        )
        for which, first, block, there, columns in PIECES
    ]
    for block, first, end in ROW_PADS:
        own_w[block, first:end, :] = jnp.zeros((end - first, WIDE), BF)
    loads[3].wait()
    xt_own[...] = x_ref[...].astype(F32).T.astype(BF)
    xt_rows = pl.ds(pl.multiple_of(x * WIDE, WIDE), WIDE)
    xt_cols = pl.ds(pl.multiple_of(y * TB, 128), TB)
    xt_x = [send(xt_own, xt.at[xt_rows, xt_cols], at(x_=turn(x, o, NX))) for o in (1, 2, 3)]
    xt_local = local(xt_own, xt.at[xt_rows, xt_cols])
    gated(1)
    swap(1)
    swapped[0][0][1].wait_recv()
    for way in (1, -1):
        pass_on(0, way)
    gated(2)
    for m in (2, 3):
        swapped[0][0][m].wait_recv()
    swapped[0][1].wait()
    for way in (1, -1):
        pass_on(1, way)
    for copy in xt_x:
        copy.wait_recv()
    xt_local.wait()
    xt_y = [send(xt.at[:, xt_cols], xt.at[:, xt_cols], at(y_=turn(y, o, NY))) for o in (1, 2, 3)]
    for load in w_loads:
        load.wait()

    w_half = pl.ds(pl.multiple_of(c * (XB // 2), 64), XB // 2)
    w_cols = pl.ds(pl.multiple_of(x * WIDE, WIDE), WIDE)
    w_sent = [
        send(
            own_w.at[turn(x, o, NX), w_half], w_all.at[w_half, w_cols], at(x_=turn(x, o, NX))
        )
        for o in (1, 2, 3)
    ]
    w_local = local(own_w.at[x, w_half], w_all.at[w_half, w_cols])
    swap(2)

    def weight_piece(k, lo):
        n = min(256, CHUNKS[k] - lo)
        value = jnp.dot(xt[...], g[k][:, lo:lo + n], preferred_element_type=F32).astype(BF)
        for b in range(NX):
            for h in range(NC):
                wp[k][h, b * HALF:(b + 1) * HALF, lo:lo + n] = value[
                    b * WIDE + h * HALF:b * WIDE + (h + 1) * HALF
                ]

    exchanged = {}

    def exchange(k):
        exchanged[k] = send(wp[k].at[1 - c], wr[k], at(c_=1 - c))

    returned = []

    def give_back(k):
        exchanged[k].wait_recv()
        ws[k][...] = (wp[k][c].astype(F32) + wr[k][...].astype(F32)).astype(BF)
        cols = pl.ds(STARTS[k], CHUNKS[k])

        def rows(of):
            return pl.ds(pl.multiple_of(of * HALF, HALF), HALF)

        for o in (1, 2, 3):
            to = turn(x, o, NX)
            returned.append(send(ws[k].at[rows(to)], w_out.at[x, :, cols], at(x_=to)).wait_recv)
        returned.append(local(ws[k].at[rows(x)], w_out.at[x, :, cols]).wait)

    partial, scattered = {}, []

    def rows_of(b):
        return pl.ds(pl.multiple_of(turn(z, b, NZ) * ZB, 64), ZB)

    def input_part(b):
        rows = rows_of(b)
        total = None
        for k in range(len(CHUNKS)):
            term = jnp.dot(
                g[k][rows, :], w_all[STARTS[k]:STARTS[k] + CHUNKS[k], :],
                preferred_element_type=F32,
            )
            total = term if total is None else total + term
        for b_ in range(NX):
            part[b_, rows, :] = total[:, b_ * WIDE:(b_ + 1) * WIDE].astype(BF)
        partial[b] = [
            send(part.at[turn(x, o, NX), rows], part_in.at[o - 1, rows], at(x_=turn(x, o, NX)))
            for o in (1, 2, 3)
        ]

    def input_sum(b):
        rows = rows_of(b)
        for copy in partial[b]:
            copy.wait_recv()
        total = part[x, rows, :].astype(F32)
        for o in range(3):
            total = total + part_in[o, rows, :].astype(F32)
        summed[rows, :] = total.astype(BF)
        block = turn(z, b, NZ)
        owner, parity = block // 2, lax.rem(block, 2)
        away = turn(owner - y, 0, NY)
        copy = pltpu.make_async_remote_copy(
            src_ref=summed.at[rows],
            dst_ref=summed_in.at[lax.rem(away + 3, NY), pl.ds(pl.multiple_of(parity * ZB, 64), ZB)],
            send_sem=y_send.at[b + 3], recv_sem=y_recv.at[2 * away + parity],
            device_id=at(y_=owner), device_id_type=pl.DeviceIdType.MESH,
        )
        scattered.append((away, copy))

        @pl.when(away != 0)
        def _():
            copy.start()

    over_core = []
    parts_at = {(1, 6): (0,), (2, 1): (-1, 1), (2, 3): (-2, 2), (2, 5): (-3, 3), (2, 6): (4,)}
    sums_at = {(2, 1): (0,), (2, 4): (-1, 1)}
    for k in range(len(CHUNKS)):
        for e in range(events):
            if e == 4 and k < last:
                arrived(k + 1)
            for way in (1, -1):
                for copy in moved[way][k * events + e]:
                    copy.wait_recv()
                pass_on(k * events + e + 2, way)
            if (k, e) == (1, 2):
                for copy in xt_y:
                    copy.wait_recv()
            if (k, e) == (1, 4):
                for copy in w_sent:
                    copy.wait_recv()
                w_local.wait()
                over_core.append(send(w_all.at[w_half], w_all.at[w_half], at(c_=1 - c)))
            if (k, e) == (1, 6):
                over_core[0].wait_recv()
            for b in parts_at.get((k, e), ()):
                input_part(b)
            if k >= 1:
                piece = e - (2 if k == 1 else 0)
                if 0 <= piece < 3 and piece * 256 < CHUNKS[k - 1]:
                    weight_piece(k - 1, piece * 256)
                if piece == 2:
                    exchange(k - 1)
                if piece == (4 if k == 1 else 3):
                    give_back(k - 1)
            for b in sums_at.get((k, e), ()):
                input_sum(b)

    for lo in range(0, CHUNKS[last], 256):
        weight_piece(last, lo)
    exchange(last)
    for b in (-2, 2):
        input_sum(b)
    give_back(last)
    for b in (-3, 3, 4):
        input_sum(b)

    for o in (1, 2, 3):
        for parity in (0, 1):
            landed = summed_in.at[o - 1, pl.ds(parity * ZB, ZB)]
            pltpu.make_async_remote_copy(
                src_ref=landed, dst_ref=landed,
                send_sem=y_send.at[0], recv_sem=y_recv.at[2 * o + parity],
                device_id=at(y_=turn(y, o, NY)), device_id_type=pl.DeviceIdType.MESH,
            ).wait_recv()
    total = summed[pl.ds(pl.multiple_of(y * TB, 128), TB), :].astype(F32)
    for o in range(3):
        total = total + summed_in[o].astype(F32)
    ig_ref[...] = total.astype(BF)

    for wait in returned:
        wait()
    for copy in sends:
        copy.wait_send()
    for away, copy in scattered:
        pl.when(away != 0)(copy.wait_send)


def unpack(ig_in, w_out, ig_ref, go_ref, uo_ref):
    ig_ref[...] = ig_in[...]
    for which, first, block, there, columns in PIECES:
        target = (go_ref, uo_ref)[which]
        target[:, first:first + columns] = w_out[block, :, there:there + columns]


def on_device(layer_input, gate_pre, up_pre, hidden_grad, gate_weight, up_weight):
    vmem = pltpu.VMEM
    scratch = [vmem((TB, WIDE), BF)] + [vmem((ROWS, UNITS), BF)] * 3 + [vmem((NX, ROWS, XB), BF)]
    scratch += [vmem((LAYER, w), BF) for w in CHUNKS]
    scratch += [
        vmem((NX, XB, WIDE), BF),
        vmem((XB, DB), BF),
        vmem((WIDE, TB), BF),
        vmem((DB, LAYER), BF),
        vmem((NX, LAYER, WIDE), BF),
        vmem((NX - 1, LAYER, WIDE), BF),
        vmem((LAYER, WIDE), BF),
        vmem((NY, TB, WIDE), BF),
    ]
    scratch += [vmem((NC, NX * HALF, w), BF) for w in CHUNKS]
    scratch += [vmem((NX * HALF, w), BF) for w in CHUNKS]
    scratch += [vmem((NX * HALF, w), BF) for w in CHUNKS]
    scratch += [
        pltpu.SemaphoreType.DMA((N_COPIES,)),
        pltpu.SemaphoreType.DMA((N_COPIES,)),
        pltpu.SemaphoreType.DMA((20,)),
        pltpu.SemaphoreType.DMA((NZ,)),
        pltpu.SemaphoreType.DMA((2 * NY,)),
    ]
    in_vmem = pl.BlockSpec(memory_space=pltpu.VMEM)
    anywhere = pl.BlockSpec(memory_space=pl.ANY)
    input_grad, packed = pl.pallas_call(
        kernel,
        out_shape=(
            jax.ShapeDtypeStruct((TB, WIDE), BF),
            jax.ShapeDtypeStruct((NX, HALF, XB), BF),
        ),
        in_specs=[anywhere] * 6,
        out_specs=(in_vmem, anywhere),
        scratch_shapes=scratch,
        compiler_params=pltpu.CompilerParams(
            collective_id=0, has_side_effects=True, vmem_limit_bytes=56 * 1024 * 1024
        ),
    )(layer_input, gate_pre, up_pre, hidden_grad, gate_weight.T, up_weight.T)
    return pl.pallas_call(
        unpack,
        out_shape=(
            jax.ShapeDtypeStruct((TB, WIDE), BF),
            jax.ShapeDtypeStruct((HALF, UNITS), BF),
            jax.ShapeDtypeStruct((HALF, UNITS), BF),
        ),
        grid=(2,),
        in_specs=[
            pl.BlockSpec((TB // 2, WIDE), lambda i: (i, 0)),
            pl.BlockSpec((NX, HALF // 2, XB), lambda i: (0, i, 0)),
        ],
        out_specs=(
            pl.BlockSpec((TB // 2, WIDE), lambda i: (i, 0)),
            pl.BlockSpec((HALF // 2, UNITS), lambda i: (i, 0)),
            pl.BlockSpec((HALF // 2, UNITS), lambda i: (i, 0)),
        ),
    )(input_grad, packed)


def solution(mesh):
    placed = (
        P(("depth", "col"), "row"),
        P(("depth", "row"), "col"),
        P(("depth", "row"), "col"),
        P(("depth", "row"), "col"),
        P("row", "col"),
        P("row", "col"),
    )
    return jax.shard_map(
        on_device,
        mesh=mesh,
        in_specs=placed,
        out_specs=(
            P(("depth", "col"), "row"),
            P(("row", "depth"), "col"),
            P(("row", "depth"), "col"),
        ),
        check_vma=False,
    )
```

```python
import jax
import jax.numpy as jnp
from jax import lax
from jax.experimental import pallas as pl
from jax.experimental.pallas import tpu as pltpu
from jax.sharding import PartitionSpec as P

NX, NY, NZ, NC = 4, 4, 8, 2
ROWS = 48
ZB = NX * ROWS
LAYER = NZ * ZB
UNITS = 3696
XB = 1920
TILES = 29
WIDE = 128
DB = NX * WIDE
TB = 2 * ZB
HALF = WIDE // 2
CHUNKS = (640, 512, 768)
STARTS = (0, 640, 1152)
N_COPIES = 112
BF, F32 = jnp.bfloat16, jnp.float32

PIECES = (
    (0, 0, 0, 0, 1920),
    (0, 1920, 1, 0, 1776),
    (1, 0, 1, 1792, 128),
    (1, 128, 2, 0, 1920),
    (1, 2048, 3, 0, 1648),
)
PADS = ((1, 1664, 1792), (3, 1536, 1920))
ROW_PADS = ((1, 1776, 1792), (3, 1648, 1920))


def kernel(
    x_hbm, gate_hbm, up_hbm, grad_hbm, gw_hbm, uw_hbm,
    ig_ref, w_out,
    x_ref, gate_ref, up_ref, grad_ref, own_g, g0, g1, g2, own_w, w_all, xt_own, xt, part, part_in, summed, summed_in,
    wp0, wp1, wp2, wr0, wr1, wr2, ws0, ws1, ws2,
    send_sem, recv_sem, local_sem, y_send, y_recv,
):
    row, y, c = lax.axis_index("row"), lax.axis_index("col"), lax.axis_index("depth")
    z, x = row // NX, lax.rem(row, NX)
    g, wp, wr, ws = (g0, g1, g2), (wp0, wp1, wp2), (wr0, wr1, wr2), (ws0, ws1, ws2)
    last = len(CHUNKS) - 1

    def at(x_=x, y_=y, z_=z, c_=c):
        return (z_ * NX + x_, y_, c_)

    def turn(value, by, n):
        return lax.rem(value + (by + n), n)

    sends, locals_ = [], []

    def send(src, dst, device):
        i = len(sends)
        copy = pltpu.make_async_remote_copy(
            src_ref=src, dst_ref=dst, send_sem=send_sem.at[i], recv_sem=recv_sem.at[i],
            device_id=device, device_id_type=pl.DeviceIdType.MESH,
        )
        copy.start()
        sends.append(copy)
        return copy

    def local(src, dst):
        copy = pltpu.make_async_copy(src, dst, local_sem.at[len(locals_)])
        copy.start()
        locals_.append(copy)
        return copy

    loads = [
        local(src, dst)
        for src, dst in ((gate_hbm, gate_ref), (up_hbm, up_ref), (grad_hbm, grad_ref), (x_hbm, x_ref))
    ]
    partners = [at(x_=turn(x, o, NX)) for o in (1, 2, 3)]
    partners += [at(y_=turn(y, o, NY)) for o in (1, 2, 3)]
    partners += [at(z_=turn(z, o, NZ)) for o in (1, -1)]
    partners += [at(c_=1 - c)]
    barrier = pltpu.get_barrier_semaphore()
    for device in partners:
        pl.semaphore_signal(barrier, inc=1, device_id=device, device_id_type=pl.DeviceIdType.MESH)

    for block, first, end in PADS:
        own_g[block, :, first:end] = jnp.zeros((ROWS, end - first), BF)
    for load in loads[:3]:
        load.wait()

    done = set()

    def gated(k):
        for t in range(TILES):
            places = [tile % (XB // WIDE) * WIDE for tile in (t, TILES + t)]
            chunks = [sum(start <= place for start in STARTS) - 1 for place in places]
            if k not in chunks or t in done:
                continue
            done.add(t)
            n = min(WIDE, UNITS - t * WIDE)
            cut = slice(t * WIDE, t * WIDE + n)
            gate = gate_ref[:, cut].astype(F32)
            grad = grad_ref[:, cut].astype(F32)
            sigma = 1.0 / (1.0 + jnp.exp(-gate))
            scaled = grad * sigma
            values = (
                scaled * up_ref[:, cut].astype(F32) * (1.0 + gate * (1.0 - sigma)), scaled * gate
            )
            for tile, value in zip((t, TILES + t), values):
                block, first = divmod(tile * WIDE, XB)
                own_g[block, :, first:first + n] = value.astype(BF)

    gated(0)
    pl.semaphore_wait(barrier, len(partners))

    def slab(of):
        return pl.ds(pl.multiple_of((z * NX + of) * ROWS, 16), ROWS)

    mates = {1: x + 1 - 2 * lax.rem(x, 2), 2: turn(x, 2, NX), 3: 3 - x}
    swapped, first_hop = [], {}

    def swap(k):
        cols = pl.ds(STARTS[k], CHUNKS[k])
        for way in (1, -1):
            first_hop[k, way] = send(
                own_g.at[x, :, cols], g[k].at[slab(x)], at(z_=turn(z, way, NZ))
            )
        copies = {}
        for m in (1, 3, 2):
            copies[m] = send(own_g.at[mates[m], :, cols], g[k].at[slab(x)], at(x_=mates[m]))
        swapped.append((copies, local(own_g.at[x, :, cols], g[k].at[slab(x)])))

    def arrived(k):
        copies, copy = swapped[k]
        for m in (1, 2, 3):
            copies[m].wait_recv()
        copy.wait()

    near, far = [(h, s) for h in (1, 2, 3) for s in (0, 1)], [(h, s) for h in (1, 2, 3) for s in (1, 0)]
    items = {1: [], -1: [(0, h, s) for h, s in near]}
    for k in range(len(CHUNKS)):
        items[1] += [(k, h, s) for h, s in near + [(4, 0)]]
        if k:
            items[-1] += [(k, h, s) for h, s in far + [(4, 1)]]
    items[-1].insert(7, (0, 4, 1))
    events = 7
    moved = {1: [], -1: []}

    def pass_on(i, way):
        if i >= len(items[way]):
            return
        k, hop, half = items[way][i]
        to = at(z_=turn(z, way, NZ))
        if (hop, half) == (1, 0):
            rows = slab(mates[1])
            moved[way].append((first_hop[k, way], send(g[k].at[rows], g[k].at[rows], to)))
            return
        block = turn(z, -way * (hop - 1), NZ)
        part_ = x // 2 if half == 0 else 1 - x // 2
        rows = pl.ds(pl.multiple_of(block * ZB + part_ * (ZB // 2), 16), ZB // 2)
        moved[way].append((send(g[k].at[rows], g[k].at[rows], to),))

    swap(0)
    w_loads = [
        local(
            (gw_hbm, uw_hbm)[which].at[pl.ds(first, columns)],
            own_w.at[block, pl.ds(there, columns)],
        )
        for which, first, block, there, columns in PIECES
    ]
    for block, first, end in ROW_PADS:
        own_w[block, first:end, :] = jnp.zeros((end - first, WIDE), BF)
    loads[3].wait()
    xt_own[...] = x_ref[...].astype(F32).T.astype(BF)
    xt_rows = pl.ds(pl.multiple_of(x * WIDE, WIDE), WIDE)
    xt_cols = pl.ds(pl.multiple_of(y * TB, 128), TB)
    xt_x = [send(xt_own, xt.at[xt_rows, xt_cols], at(x_=turn(x, o, NX))) for o in (1, 2, 3)]
    xt_local = local(xt_own, xt.at[xt_rows, xt_cols])
    gated(1)
    swap(1)
    swapped[0][0][1].wait_recv()
    for way in (1, -1):
        pass_on(0, way)
    gated(2)
    for m in (2, 3):
        swapped[0][0][m].wait_recv()
    swapped[0][1].wait()
    for way in (1, -1):
        pass_on(1, way)
    for copy in xt_x:
        copy.wait_recv()
    xt_local.wait()
    xt_y = [send(xt.at[:, xt_cols], xt.at[:, xt_cols], at(y_=turn(y, o, NY))) for o in (1, 2, 3)]
    for load in w_loads:
        load.wait()

    w_half = pl.ds(pl.multiple_of(c * (XB // 2), 64), XB // 2)
    w_cols = pl.ds(pl.multiple_of(x * WIDE, WIDE), WIDE)
    w_sent = [
        send(
            own_w.at[turn(x, o, NX), w_half], w_all.at[w_half, w_cols], at(x_=turn(x, o, NX))
        )
        for o in (1, 2, 3)
    ]
    w_local = local(own_w.at[x, w_half], w_all.at[w_half, w_cols])
    swap(2)

    def weight_piece(k, lo):
        n = min(256, CHUNKS[k] - lo)
        value = jnp.dot(xt[...], g[k][:, lo:lo + n], preferred_element_type=F32).astype(BF)
        for b in range(NX):
            for h in range(NC):
                wp[k][h, b * HALF:(b + 1) * HALF, lo:lo + n] = value[
                    b * WIDE + h * HALF:b * WIDE + (h + 1) * HALF
                ]

    exchanged = {}

    def exchange(k):
        exchanged[k] = send(wp[k].at[1 - c], wr[k], at(c_=1 - c))

    returned = []

    def give_back(k):
        exchanged[k].wait_recv()
        ws[k][...] = (wp[k][c].astype(F32) + wr[k][...].astype(F32)).astype(BF)
        cols = pl.ds(STARTS[k], CHUNKS[k])

        def rows(of):
            return pl.ds(pl.multiple_of(of * HALF, HALF), HALF)

        for o in (1, 2, 3):
            to = turn(x, o, NX)
            returned.append(send(ws[k].at[rows(to)], w_out.at[x, :, cols], at(x_=to)).wait_recv)
        returned.append(local(ws[k].at[rows(x)], w_out.at[x, :, cols]).wait)

    partial, scattered = {}, []

    def rows_of(b):
        return pl.ds(pl.multiple_of(turn(z, b, NZ) * ZB, 64), ZB)

    def input_part(b):
        rows = rows_of(b)
        total = None
        for k in range(len(CHUNKS)):
            term = jnp.dot(
                g[k][rows, :], w_all[STARTS[k]:STARTS[k] + CHUNKS[k], :],
                preferred_element_type=F32,
            )
            total = term if total is None else total + term
        for b_ in range(NX):
            part[b_, rows, :] = total[:, b_ * WIDE:(b_ + 1) * WIDE].astype(BF)
        partial[b] = [
            send(part.at[turn(x, o, NX), rows], part_in.at[o - 1, rows], at(x_=turn(x, o, NX)))
            for o in (1, 2, 3)
        ]

    def input_sum(b):
        rows = rows_of(b)
        for copy in partial[b]:
            copy.wait_recv()
        total = part[x, rows, :].astype(F32)
        for o in range(3):
            total = total + part_in[o, rows, :].astype(F32)
        summed[rows, :] = total.astype(BF)
        block = turn(z, b, NZ)
        owner, parity = block // 2, lax.rem(block, 2)
        away = turn(owner - y, 0, NY)
        copy = pltpu.make_async_remote_copy(
            src_ref=summed.at[rows],
            dst_ref=summed_in.at[lax.rem(away + 3, NY), pl.ds(pl.multiple_of(parity * ZB, 64), ZB)],
            send_sem=y_send.at[b + 3], recv_sem=y_recv.at[2 * away + parity],
            device_id=at(y_=owner), device_id_type=pl.DeviceIdType.MESH,
        )
        scattered.append((away, copy))

        @pl.when(away != 0)
        def _():
            copy.start()

    over_core = []
    parts_at = {(1, 6): (0,), (2, 1): (-1, 1), (2, 3): (-2, 2), (2, 5): (-3, 3), (2, 6): (4,)}
    sums_at = {(2, 1): (0,), (2, 4): (-1, 1)}
    for k in range(len(CHUNKS)):
        for e in range(events):
            if e == 4 and k < last:
                arrived(k + 1)
            for way in (1, -1):
                for copy in moved[way][k * events + e]:
                    copy.wait_recv()
                pass_on(k * events + e + 2, way)
            if (k, e) == (1, 2):
                for copy in xt_y:
                    copy.wait_recv()
            if (k, e) == (1, 4):
                for copy in w_sent:
                    copy.wait_recv()
                w_local.wait()
                over_core.append(send(w_all.at[w_half], w_all.at[w_half], at(c_=1 - c)))
            if (k, e) == (1, 6):
                over_core[0].wait_recv()
            for b in parts_at.get((k, e), ()):
                input_part(b)
            if k >= 1:
                piece = e - (2 if k == 1 else 0)
                if 0 <= piece < 3 and piece * 256 < CHUNKS[k - 1]:
                    weight_piece(k - 1, piece * 256)
                if piece == (2 if k == 1 else 1):
                    exchange(k - 1)
                if piece == (4 if k == 1 else 2):
                    give_back(k - 1)
            for b in sums_at.get((k, e), ()):
                input_sum(b)

    for lo in range(0, CHUNKS[last], 256):
        weight_piece(last, lo)
    exchange(last)
    for b in (-2, 2):
        input_sum(b)
    give_back(last)
    for b in (-3, 3, 4):
        input_sum(b)

    for o in (1, 2, 3):
        for parity in (0, 1):
            landed = summed_in.at[o - 1, pl.ds(parity * ZB, ZB)]
            pltpu.make_async_remote_copy(
                src_ref=landed, dst_ref=landed,
                send_sem=y_send.at[0], recv_sem=y_recv.at[2 * o + parity],
                device_id=at(y_=turn(y, o, NY)), device_id_type=pl.DeviceIdType.MESH,
            ).wait_recv()
    total = summed[pl.ds(pl.multiple_of(y * TB, 128), TB), :].astype(F32)
    for o in range(3):
        total = total + summed_in[o].astype(F32)
    ig_ref[...] = total.astype(BF)

    for wait in returned:
        wait()
    for copy in sends:
        copy.wait_send()
    for away, copy in scattered:
        pl.when(away != 0)(copy.wait_send)


def unpack(ig_in, w_out, ig_ref, go_ref, uo_ref):
    ig_ref[...] = ig_in[...]
    for which, first, block, there, columns in PIECES:
        target = (go_ref, uo_ref)[which]
        target[:, first:first + columns] = w_out[block, :, there:there + columns]


def on_device(layer_input, gate_pre, up_pre, hidden_grad, gate_weight, up_weight):
    vmem = pltpu.VMEM
    scratch = [vmem((TB, WIDE), BF)] + [vmem((ROWS, UNITS), BF)] * 3 + [vmem((NX, ROWS, XB), BF)]
    scratch += [vmem((LAYER, w), BF) for w in CHUNKS]
    scratch += [
        vmem((NX, XB, WIDE), BF),
        vmem((XB, DB), BF),
        vmem((WIDE, TB), BF),
        vmem((DB, LAYER), BF),
        vmem((NX, LAYER, WIDE), BF),
        vmem((NX - 1, LAYER, WIDE), BF),
        vmem((LAYER, WIDE), BF),
        vmem((NY, TB, WIDE), BF),
    ]
    scratch += [vmem((NC, NX * HALF, w), BF) for w in CHUNKS]
    scratch += [vmem((NX * HALF, w), BF) for w in CHUNKS]
    scratch += [vmem((NX * HALF, w), BF) for w in CHUNKS]
    scratch += [
        pltpu.SemaphoreType.DMA((N_COPIES,)),
        pltpu.SemaphoreType.DMA((N_COPIES,)),
        pltpu.SemaphoreType.DMA((20,)),
        pltpu.SemaphoreType.DMA((NZ,)),
        pltpu.SemaphoreType.DMA((2 * NY,)),
    ]
    in_vmem = pl.BlockSpec(memory_space=pltpu.VMEM)
    anywhere = pl.BlockSpec(memory_space=pl.ANY)
    input_grad, packed = pl.pallas_call(
        kernel,
        out_shape=(
            jax.ShapeDtypeStruct((TB, WIDE), BF),
            jax.ShapeDtypeStruct((NX, HALF, XB), BF),
        ),
        in_specs=[anywhere] * 6,
        out_specs=(in_vmem, anywhere),
        scratch_shapes=scratch,
        compiler_params=pltpu.CompilerParams(
            collective_id=0, has_side_effects=True, vmem_limit_bytes=56 * 1024 * 1024
        ),
    )(layer_input, gate_pre, up_pre, hidden_grad, gate_weight.T, up_weight.T)
    return pl.pallas_call(
        unpack,
        out_shape=(
            jax.ShapeDtypeStruct((TB, WIDE), BF),
            jax.ShapeDtypeStruct((HALF, UNITS), BF),
            jax.ShapeDtypeStruct((HALF, UNITS), BF),
        ),
        grid=(2,),
        in_specs=[
            pl.BlockSpec((TB // 2, WIDE), lambda i: (i, 0)),
            pl.BlockSpec((NX, HALF // 2, XB), lambda i: (0, i, 0)),
        ],
        out_specs=(
            pl.BlockSpec((TB // 2, WIDE), lambda i: (i, 0)),
            pl.BlockSpec((HALF // 2, UNITS), lambda i: (i, 0)),
            pl.BlockSpec((HALF // 2, UNITS), lambda i: (i, 0)),
        ),
    )(input_grad, packed)


def solution(mesh):
    placed = (
        P(("depth", "col"), "row"),
        P(("depth", "row"), "col"),
        P(("depth", "row"), "col"),
        P(("depth", "row"), "col"),
        P("row", "col"),
        P("row", "col"),
    )
    return jax.shard_map(
        on_device,
        mesh=mesh,
        in_specs=placed,
        out_specs=(
            P(("depth", "col"), "row"),
            P(("row", "depth"), "col"),
            P(("row", "depth"), "col"),
        ),
        check_vma=False,
    )
```
